128 devices in a mesh: grp: 4 (over z), tp: 32 (over y, x, core).
Axes of the slice: x: 4, y: 4, z: 4, core: 2. Of those that a mesh axis runs over, the one named last changes fastest.
Arguments:
- hidden_in: bfloat16 [512, 7168], P(('grp', 'tp')), may hold values from -3 to 3
- queries: bfloat16 [512, 128, 576], P(('grp', 'tp')), may hold values from -15 to 15
- cache: bfloat16 [524288, 576], P(('grp', 'tp')), may hold values from -6 to 6
- lengths: int32 [512], P(('grp', 'tp')), may hold values from 16 to 1024, as said below
- value_up: bfloat16 [128, 512, 128], P('tp'), may hold values from -0.25 to 0.25
- out_proj: bfloat16 [16384, 7168], P('tp'), may hold values from -0.046875 to 0.046875
- norm_gain: float32 [7168], replicated, may hold values from 0.1 to 1.9
- routes: int32 [512, 8], P(('grp', 'tp')), may hold values from 0 to 31, all different within a row; in each aligned block of 4 rows (0 to 3, 4 to 7, ...) at most 3 rows name the same one
- route_weight: float32 [512, 8], P(('grp', 'tp')), may hold values from 0.1 to 1
- w_gate: bfloat16 [32, 7168, 1024], P('tp', None, 'grp'), may hold values from -0.0625 to 0.0625
- w_up: bfloat16 [32, 7168, 1024], P('tp', None, 'grp'), may hold values from -0.0625 to 0.0625
- w_down: bfloat16 [32, 1024, 7168], P('tp', 'grp'), may hold values from -0.1875 to 0.1875
Outputs:
- layer_out: bfloat16 [512, 7168], P(('grp', 'tp'))
The draws below stay inside these ranges and needn't reach their ends.
Inputs may be any that keep to these rules, and one draw needn't show every extreme that they name: Token i's cached rows are positions start_i to start_i + lengths[i] - 1 of its device's 4096 rows, start_i being the sum of the earlier lengths of that device; each device's lengths sum to at most 4096, and on some device to exactly 4096. Rows past a device's sum are unused. `routes`: each row names 8 different experts; within the 4 rows of one device no expert is named more than 3 times.
All inputs are finite; a program needn't handle non-finite values.
Results may differ from the reference program's by a relative error of at most 0.028.
Values may be sent and summed in bfloat16 or wider, within the bound.
No kernel may reach another device: no remote copies, remote signals or barrier semaphores. Data moves between devices by JAX's collectives and lax.ppermute only.
A program may use at most 128 MiB of HBM per device.

```python
import math
import jax
import jax.numpy as jnp
import numpy as np
from jax import lax

D = 7168
H = 128
LAT = 512
ROPE = 64
DV = 128
TOP = 8
FF = 1024
REQ_DEV = 4
POOL = 4096
EXPERTS = 32
CAP = 3
TOKENS = 512
CTX = 524288
N_GRP = 4
N_TP = 32


def draw_cache(key, part):
    key = jax.random.fold_in(key, 21)
    full_shape = (N_GRP * N_TP, POOL, LAT + ROPE)
    values = jnp.clip(jax.random.normal(key, full_shape, jnp.float32), -6.0, 6.0)
    return values.reshape(CTX, LAT + ROPE).astype(jnp.bfloat16)


def draw_queries(key, part):
    key = jax.random.fold_in(key, 31)
    main_key = jax.random.fold_in(key, 0)
    full_shape = (TOKENS, H, LAT + ROPE)
    values = 2.0 * jnp.clip(jax.random.normal(main_key, full_shape, jnp.float32), -6.0, 6.0)
    return values.astype(jnp.bfloat16)


def draw_lengths(key, part):
    key = jax.random.fold_in(key, 11)
    heavy_key, long_key, short_key, full_key, least_key = jax.random.split(key, 5)
    device_count = N_GRP * N_TP
    longest = POOL // REQ_DEV
    shortest = max(2, longest // 64)
    light_top = max(shortest + 1, longest * 3 // 8)
    heavy = jax.random.randint(heavy_key, (device_count,), 0, 4) == 0
    long_lengths = jax.random.randint(long_key, (device_count, REQ_DEV), shortest, longest + 1)
    short_lengths = jax.random.randint(short_key, (device_count, REQ_DEV), shortest, light_top + 1)
    chosen = jnp.where(heavy[:, None], long_lengths, short_lengths)
    full_device = jax.random.randint(full_key, (), 0, device_count)
    device_ids = jnp.arange(device_count)
    chosen = jnp.where((device_ids == full_device)[:, None], longest, chosen)
    least_device = (full_device + 1 + jax.random.randint(least_key, (), 0, device_count - 1)) % device_count
    request_ids = jnp.arange(REQ_DEV)
    least_mask = (device_ids == least_device)[:, None] & (request_ids == 0)[None, :]
    chosen = jnp.where(least_mask, shortest, chosen)
    return chosen.reshape(-1).astype(jnp.int32)


def level_of(rng, shape, pieces, least, high):
    def one(position, parts):
        heights = jax.random.uniform(jax.random.fold_in(jax.random.fold_in(rng, 6), position), (parts,), jnp.float32, least / len(pieces), high / len(pieces))
        return jnp.repeat(jnp.exp(heights), shape[position] // parts).reshape((-1,) + (1,) * (len(shape) - position - 1))

    level = one(*pieces[0])
    for cut in pieces[1:]:
        level = level * one(*cut)
    return level


def shared_out(key, own, number, rows, count, top, most, slope):
    order = jax.random.permutation(key, count)
    packed, ordinary = portions_of(count, rows * top, most, slope, True), portions_of(count, rows * top, most, slope, False)
    places = jnp.arange(count)

    def named(tallies, turn):
        used = int((tallies > 0).sum())
        fixed = max(1, used // 4)
        shifted = fixed + (places - fixed + turn * (used - fixed)) % max(1, count - fixed)
        return jnp.zeros((count,), jnp.int32).at[order[jnp.where(places < fixed, places, shifted)]].set(jnp.asarray(tallies, jnp.int32))

    tallies = jnp.where(number % 4 == 0, named(packed, number // 4), named(ordinary, number - number // 4 - 1))
    mixed = jax.random.permutation(jax.random.fold_in(own, 3), count)
    giver, receiver = mixed[0:count // 2 * 2:2], mixed[1:count // 2 * 2:2]
    slack = jnp.minimum(tallies[giver] - 1, most - tallies[receiver]) // 2
    slack = jnp.where((giver == order[0]) | (receiver == order[0]) | (tallies[receiver] == 0), 0, jnp.maximum(slack, 0))
    shifted = jax.random.randint(jax.random.fold_in(own, 4), (count // 2,), 0, 1 << 20) % (slack + 1)
    tallies = tallies.at[giver].add(-shifted).at[receiver].add(shifted)
    labels = jnp.searchsorted(jnp.cumsum(tallies), jnp.arange(rows * top), side="right").astype(jnp.int32)
    grid = labels.reshape(top, rows).T
    grid = grid[jax.random.permutation(jax.random.fold_in(own, 1), rows)]
    turn = jax.random.randint(jax.random.fold_in(own, 2), (rows, 1), 0, top)
    return jnp.take_along_axis(grid, (jnp.arange(top)[None, :] + turn) % top, axis=1)


def portions_of(count, total, reach, skew, full):
    portions = [(1 << 20) // math.isqrt(rank ** skew) + 1 for rank in range(1, count + 1)]
    largest = reach if full else min(reach, max(-(-total // count), total * portions[0] // sum(portions)))
    least = 1 if total - largest >= count - 1 else 0
    given, rest = [largest] + [least] * (count - 1), total - largest - least * (count - 1)
    while rest > 0:
        candidates = [i for i in range(1, count) if given[i] < largest] or [i for i in range(1, count) if given[i] < reach]
        whole, budget = sum([portions[i] for i in candidates]), rest
        for i in candidates:
            more = min(reach - given[i], max(1, budget * portions[i] // whole), rest)
            given[i] = given[i] + more
            rest = rest - more
    return np.array(given)


def scatter_about(own_key, dims, spread, bound, cuts=(), kind=jnp.bfloat16):
    result = jax.random.normal(own_key, dims, jnp.float32) * spread
    if len(cuts) > 0:
        result = level_of(own_key, dims, cuts, -0.22, 0.18) * result
    return jnp.clip(result, min=-bound, max=bound).astype(kind)


def setup_inputs(seed: int = 0) -> dict:
    seeds = jax.random.split(jax.random.key(seed), 13)
    hidden_in = scatter_about(seeds[0], (TOKENS, D), 0.5, 3.0, ((0, 128),))
    queries = draw_queries(jax.random.fold_in(seeds[12], 71), 0)
    cache = draw_cache(jax.random.fold_in(seeds[12], 71), 0)
    lengths = draw_lengths(jax.random.fold_in(seeds[12], 71), 0)
    value_up = scatter_about(seeds[4], (H, LAT, DV), LAT ** -0.5, 0.25, ((0, 32),))
    out_proj = scatter_about(seeds[5], (H * DV, D), (H * DV) ** -0.5, 0.046875, ((0, 32),))
    norm_gain = jnp.clip(1.0 + 0.18 * jax.random.normal(seeds[6], (D,), jnp.float32), 0.1, 1.9)
    routes_keys = jax.random.split(jax.random.fold_in(seeds[7], 1), TOKENS // REQ_DEV)
    routes_turns = jax.random.permutation(jax.random.fold_in(seeds[7], 3), TOKENS // REQ_DEV)
    routes = jax.vmap(lambda own, number: shared_out(jax.random.fold_in(seeds[7], 2), own, number, REQ_DEV, EXPERTS, TOP, CAP, 2))(routes_keys, routes_turns).reshape((TOKENS, TOP))
    route_weight = jnp.clip(jnp.exp(math.log(1.0) - 2.3025851 * jax.random.uniform(seeds[8], (TOKENS, TOP), jnp.float32) ** level_of(seeds[8], (TOKENS, TOP), ((0, 128),), -0.2, 0.2)), 0.1, 1.0)
    w_gate = scatter_about(seeds[9], (EXPERTS, D, FF), D ** -0.5, 0.0625, ((0, 32), (2, 4)))
    w_up = scatter_about(seeds[10], (EXPERTS, D, FF), D ** -0.5, 0.0625, ((0, 32), (2, 4)))
    w_down = scatter_about(seeds[11], (EXPERTS, FF, D), FF ** -0.5, 0.1875, ((0, 32), (1, 4)))
    return dict(hidden_in=hidden_in, queries=queries, cache=cache, lengths=lengths, value_up=value_up, out_proj=out_proj, norm_gain=norm_gain, routes=routes, route_weight=route_weight, w_gate=w_gate, w_up=w_up, w_down=w_down)


tile_rows = 64

def attend_all(queries, cache, lengths):
    width_all = LAT + ROPE
    device_count = N_GRP * N_TP
    longest = POOL // REQ_DEV
    score_scale = (DV + ROPE) ** (-0.5)
    query_blocks = queries.reshape(device_count, REQ_DEV, H, width_all)
    cache_blocks = cache.reshape(device_count, POOL, width_all)
    length_blocks = lengths.reshape(device_count, REQ_DEV)

    def device_attention(operands):
        device_queries, device_cache, device_lengths = operands
        padded = jnp.concatenate([device_cache, jnp.zeros((longest, width_all), device_cache.dtype)], 0)
        starts = (jnp.cumsum(device_lengths) - device_lengths).astype(jnp.int32)

        def request_attention(query_rows, start_pos, length):
            key_rows = lax.dynamic_slice_in_dim(padded, start_pos.astype(jnp.int32), longest, 0)
            scores = jnp.dot(query_rows, key_rows.T, preferred_element_type=jnp.float32) * score_scale
            live_mask = jnp.arange(longest, dtype=jnp.int32) < length
            scores = jnp.where(live_mask[None, :], scores, -1e+30)
            largest = lax.optimization_barrier(jnp.max(scores, 1, keepdims=True))
            weights = jnp.where(live_mask[None, :], jnp.exp(scores - largest), 0.0)
            totals = lax.optimization_barrier(jnp.sum(weights, 1, keepdims=True))
            weighted = jnp.dot(weights.astype(jnp.bfloat16), key_rows[:, :LAT], preferred_element_type=jnp.float32)
            return (weighted / totals).astype(jnp.bfloat16)
        return jax.vmap(request_attention)(device_queries, starts, device_lengths)
    latent = lax.map(device_attention, (query_blocks, cache_blocks, length_blocks))
    return latent.reshape(TOKENS, H, LAT)

def route_experts(normed, routes, route_weight, w_gate, w_up, w_down):
    pair_count = TOKENS * TOP
    pair_expert = routes.reshape(-1).astype(jnp.int32)
    expert_ids = jnp.arange(EXPERTS, dtype=jnp.int32)
    counts = lax.optimization_barrier(jnp.sum((pair_expert[:, None] == expert_ids[None, :]).astype(jnp.int32), 0))
    padded = ((counts + tile_rows - 1) // tile_rows * tile_rows).astype(jnp.int32)
    pad_end = jnp.cumsum(padded).astype(jnp.int32)
    pad_start = pad_end - padded
    pair_order = jnp.argsort(pair_expert, stable=True).astype(jnp.int32)
    sorted_expert = pair_expert[pair_order]
    group_start = (jnp.cumsum(counts) - counts).astype(jnp.int32)
    pair_rank = jnp.arange(pair_count, dtype=jnp.int32) - group_start[sorted_expert]
    dest_slot = (pad_start[sorted_expert] + pair_rank).astype(jnp.int32)
    tile_count = pair_count // tile_rows + EXPERTS
    slot_pair = jnp.full((tile_count * tile_rows,), pair_count, jnp.int32).at[dest_slot].set(pair_order)
    tile_first = jnp.arange(tile_count, dtype=jnp.int32) * tile_rows
    tile_expert = jnp.minimum(lax.optimization_barrier(jnp.sum((tile_first[:, None] >= pad_end[None, :]).astype(jnp.int32), 1)), EXPERTS - 1).astype(jnp.int32)
    quarter = FF // N_GRP

    def run_tile(operands):
        pair_ids, expert = operands
        token_ids = jnp.where(pair_ids < pair_count, pair_ids // TOP, 0).astype(jnp.int32)
        token_rows = normed[token_ids]
        gate_act = jnp.dot(token_rows, w_gate[expert], preferred_element_type=jnp.float32)
        up_act = jnp.dot(token_rows, w_up[expert], preferred_element_type=jnp.float32)
        hidden = (jax.nn.silu(gate_act) * up_act).astype(jnp.bfloat16)
        summed = jnp.zeros((tile_rows, D), jnp.float32)
        for group_idx in range(N_GRP):
            partial_value = jnp.dot(hidden[:, group_idx * quarter:(group_idx + 1) * quarter], w_down[expert, group_idx * quarter:(group_idx + 1) * quarter], preferred_element_type=jnp.float32).astype(jnp.bfloat16)
            partial_value = lax.optimization_barrier(partial_value)
            summed = summed + partial_value.astype(jnp.float32)
        return summed.astype(jnp.bfloat16)
    tile_out = lax.map(run_tile, (slot_pair.reshape(tile_count, tile_rows), tile_expert)).reshape(-1, D)
    slot_of_pair = jnp.zeros((pair_count,), jnp.int32).at[pair_order].set(dest_slot)
    pair_out = tile_out[slot_of_pair].reshape(TOKENS, TOP, D).astype(jnp.float32)
    return lax.optimization_barrier(jnp.sum(route_weight[:, :, None] * pair_out, 1))

def reference(hidden_in, queries, cache, lengths, value_up, out_proj, norm_gain, routes, route_weight, w_gate, w_up, w_down):
    latent = attend_all(queries, cache, lengths)
    head_out = jnp.einsum('thl,hlv->thv', latent.astype(jnp.float32), value_up.astype(jnp.float32))
    head_out = head_out.astype(jnp.bfloat16).reshape(TOKENS, H * DV)
    attended = jnp.dot(head_out, out_proj, preferred_element_type=jnp.float32)
    residual = hidden_in.astype(jnp.float32) + attended
    normed = (residual * lax.rsqrt(lax.optimization_barrier(jnp.mean(residual * residual, -1, keepdims=True)) + 1e-06) * norm_gain).astype(jnp.bfloat16)
    routed = route_experts(normed, routes, route_weight, w_gate, w_up, w_down)
    return (residual + routed).astype(jnp.bfloat16)
```

```python
import jax
import jax.numpy as jnp
from jax import lax
from jax.sharding import Mesh, PartitionSpec as P

LAT = 512
ROPE = 64
DV = 128
TOP = 8
N = 4
AXES = ("z", "y", "x", "c")
PLANE = ("y", "x", "c")
BF = jnp.bfloat16
F32 = jnp.float32


def bounds(request_lengths, head_count):
    starts = jnp.cumsum(request_lengths) - request_lengths
    row_start = jnp.repeat(starts, head_count)
    row_end = jnp.repeat(starts + request_lengths, head_count)
    return (row_start, row_end)


def partial_attention(
    query_rows, key_rows, row_start, row_end, block_count, block_len, score_scale
):
    row_total = query_rows.shape[0]
    initial = (
        jnp.full((row_total,), -1e30, jnp.float32),
        jnp.zeros((row_total,), jnp.float32),
        jnp.zeros((row_total, LAT), jnp.float32),
    )

    def block_step(block_idx, carried):
        maxima, totals, weighted = carried
        block = lax.dynamic_slice_in_dim(key_rows, block_idx * block_len, block_len, 0)
        scores = (
            lax.dot_general(
                query_rows, block, (((1,), (1,)), ((), ())), preferred_element_type=jnp.float32
            )
            * score_scale
        )
        positions = block_idx * block_len + jnp.arange(block_len, dtype=jnp.int32)
        live_mask = (positions[None, :] >= row_start[:, None]) & (
            positions[None, :] < row_end[:, None]
        )
        scores = jnp.where(live_mask, scores, -1e30)
        new_maxima = jnp.maximum(maxima, jnp.max(scores, 1))
        weights = jnp.where(live_mask, jnp.exp(scores - new_maxima[:, None]), 0.0)
        rescale = jnp.exp(maxima - new_maxima)
        totals = totals * rescale + jnp.sum(weights, 1)
        weighted = weighted * rescale[:, None] + jnp.dot(
            weights.astype(jnp.bfloat16), block[:, :LAT], preferred_element_type=jnp.float32
        )
        return (new_maxima, totals, weighted)

    return lax.fori_loop(0, block_count, block_step, initial)


def attend(queries, cache, lengths):
    requests, head_count, width = queries.shape
    block_len = 512
    row_start, row_end = bounds(lengths, head_count)
    block_count = (jnp.sum(lengths) + block_len - 1) // block_len
    maxima, totals, weighted = partial_attention(
        queries.reshape(requests * head_count, width), cache, row_start, row_end,
        block_count, block_len, (DV + ROPE) ** (-0.5),
    )
    return (weighted / totals[:, None]).astype(BF).reshape(requests, head_count, LAT)


def fetch(block, axis, offset):
    return lax.ppermute(block, axis, [((i + offset) % N, i) for i in range(N)])


def push(block, axis, offset):
    return lax.ppermute(block, axis, [(i, (i + offset) % N) for i in range(N)])


def swap(block):
    return lax.ppermute(block, "c", [(0, 1), (1, 0)])


def rolled(block, shift, dim):
    return lax.dynamic_slice_in_dim(
        jnp.concatenate([block, block], dim), shift, block.shape[dim], dim
    )


def half(block, which, dim):
    size = block.shape[dim] // 2
    return lax.dynamic_slice_in_dim(block, which * size, size, dim)


def mm(a, b):
    return jnp.dot(a, b, preferred_element_type=F32)


def add_up(blocks):
    total = blocks[0].astype(F32)
    for block in blocks[1:]:
        total = total + block.astype(F32)
    return total


def scatter_axis(chunks, axis):
    arrived = [push(chunks[k], axis, k) for k in range(1, N)]
    return add_up([chunks[0]] + arrived)


def gather_axis(block, axis):
    return [block] + [fetch(block, axis, k) for k in range(1, N)]


def local(
    hidden_in, queries, cache, lengths, value_up, out_proj, norm_gain, routes, route_weight,
    w_gate, w_up, w_down,
):
    zi, yi, xi, ci = (lax.axis_index(a) for a in AXES)
    other = 1 - ci
    width = hidden_in.shape[1]
    wide = width // 2
    part = wide // 2
    requests = hidden_in.shape[0]
    chip = 2 * requests

    own_hidden = half(hidden_in, ci, 1)
    sent_hidden = swap(half(hidden_in, other, 1))
    first = jnp.where(ci == 0, own_hidden, sent_hidden)
    second = jnp.where(ci == 0, sent_hidden, own_hidden)
    chip_hidden = jnp.concatenate([first, second], 0)
    gain = lax.dynamic_slice_in_dim(norm_gain, ci * wide, wide, 0)

    experts = jnp.arange(N * N * 2, dtype=jnp.int32)
    dense = jnp.sum(
        jnp.where(routes[:, :, None] == experts, route_weight[:, :, None], 0.0), 1
    )
    dense_all = lax.all_gather(dense, AXES, axis=0, tiled=True)

    down_other = swap(half(w_down[0], other, 1))
    down_pair = jnp.concatenate([half(w_down[0], ci, 1), down_other], 0)

    latent = attend(queries, cache, lengths)
    regrouped = lax.all_to_all(latent, PLANE, split_axis=1, concat_axis=0, tiled=True)
    head_out = jnp.einsum("thl,hlv->thv", regrouped, value_up, preferred_element_type=F32)
    head_out = head_out.astype(BF).reshape(N, N, chip, -1)
    head_out = rolled(rolled(head_out, yi, 0), xi, 1)
    head_yx = head_out.reshape(N * N * chip, -1)
    sent = swap(mm(head_yx, half(out_proj, other, 1)).astype(BF))
    partial = mm(head_yx, half(out_proj, ci, 1)) + sent.astype(F32)
    partial = partial.astype(BF).reshape(N, N, chip, wide)
    first_a = scatter_axis([partial[k, :, :, :part] for k in range(N)], "y").astype(BF)
    first_b = scatter_axis([partial[:, k, :, part:] for k in range(N)], "x").astype(BF)
    attended_a = scatter_axis([first_a[k] for k in range(N)], "x")
    attended_b = scatter_axis([first_b[k] for k in range(N)], "y")
    attended = jnp.concatenate([attended_a, attended_b], 1)
    residual = chip_hidden.astype(F32) + attended
    squares = jnp.sum(residual * residual, 1, keepdims=True)
    squares = squares + swap(squares)
    normed = (residual * lax.rsqrt(squares / width + 1e-06) * gain).astype(BF)

    zed = jnp.concatenate(gather_axis(normed, "z"), 0)
    tok_a = jnp.concatenate(gather_axis(zed[:, :part], "x"), 0)
    tok_b = jnp.concatenate(gather_axis(zed[:, part:], "y"), 0)
    tok_a = jnp.concatenate(gather_axis(tok_a, "y"), 0)
    tok_b = jnp.concatenate(gather_axis(tok_b, "x"), 0)
    pair_a = swap(tok_a)
    pair_b = swap(tok_b)

    def project(weights):
        quarters = weights.reshape(2, 2, part, -1)
        mine = lax.dynamic_index_in_dim(quarters, ci, 0, keepdims=False)
        theirs = lax.dynamic_index_in_dim(quarters, other, 0, keepdims=False)
        in_yx = mm(tok_a, mine[0]) + mm(pair_a, theirs[0])
        in_xy = mm(tok_b, mine[1]) + mm(pair_b, theirs[1])
        in_xy = in_xy.reshape(N, N, N * chip, -1).swapaxes(0, 1).reshape(in_yx.shape)
        return in_yx + in_xy

    gate_act = project(w_gate[0])
    up_act = project(w_up[0])
    rank = (yi * N + xi) * 2 + ci
    mix = lax.dynamic_slice_in_dim(dense_all, rank, 1, 1).reshape(N, N, N, chip)
    mix = rolled(rolled(rolled(mix, zi, 0), yi, 1), xi, 2)
    mix = mix.transpose(1, 2, 0, 3).reshape(-1, 1)
    hidden = (jax.nn.silu(gate_act) * up_act * mix).astype(BF)
    both = jnp.concatenate([hidden, swap(hidden)], 1)
    both_yx = both.reshape(N, N * N * chip, -1)
    both_xy = both.reshape(N, N, N * chip, -1).swapaxes(0, 1).reshape(both_yx.shape)
    out_a = scatter_axis([mm(both_yx[k], down_pair[:, :part]).astype(BF) for k in range(N)], "y")
    out_b = scatter_axis([mm(both_xy[k], down_pair[:, part:]).astype(BF) for k in range(N)], "x")
    out_a = out_a.astype(BF).reshape(N, N * chip, part)
    out_b = out_b.astype(BF).reshape(N, N * chip, part)
    out_a = scatter_axis([out_a[k] for k in range(N)], "x")
    out_b = scatter_axis([out_b[k] for k in range(N)], "y")
    routed = jnp.concatenate([out_a, out_b], 1).astype(BF).reshape(N, chip, wide)
    routed = scatter_axis([routed[k] for k in range(N)], "z")
    layer_out = (residual + routed).astype(BF).reshape(2, requests, wide)
    mine = lax.dynamic_index_in_dim(layer_out, ci, 0, keepdims=False)
    theirs = swap(lax.dynamic_index_in_dim(layer_out, other, 0, keepdims=False))
    left = jnp.where(ci == 0, mine, theirs)
    right = jnp.where(ci == 0, theirs, mine)
    return jnp.concatenate([left, right], 1)


def solution(mesh):
    torus = Mesh(mesh.devices.reshape(N, N, N, 2), AXES)
    in_specs = (
        P(AXES, None),
        P(AXES, None, None),
        P(AXES, None),
        P(AXES),
        P(PLANE, None, None),
        P(PLANE, None),
        P(),
        P(AXES, None),
        P(AXES, None),
        P(PLANE, None, "z"),
        P(PLANE, None, "z"),
        P(PLANE, "z", None),
    )
    return jax.shard_map(
        local, mesh=torus, in_specs=in_specs, out_specs=P(AXES, None), check_vma=False
    )
```

```python
import functools

import jax
import jax.numpy as jnp
from jax import lax
from jax.experimental import pallas as pl
from jax.experimental.pallas import tpu as pltpu
from jax.sharding import Mesh, PartitionSpec as P

LAT = 512
ROPE = 64
DV = 128
LONGEST = 1024
ALIGN = 128
N = 4
EXPERTS = 32
EXTRA = 128
AXES = ("z", "y", "x", "c")
PLANE = ("y", "x", "c")
BF = jnp.bfloat16
F32 = jnp.float32


def attend_kernel(lengths, queries, cache, latent, window, arrived):
    requests = queries.shape[0]
    rows = window.shape[2]
    scale = (DV + ROPE) ** (-0.5)
    begins, bases, copies = [], [], []
    begin = jnp.int32(0)
    for i in range(requests):
        base = jnp.minimum(begin // ALIGN * ALIGN, cache.shape[1] - rows)
        base = pl.multiple_of(base, ALIGN)
        copy = pltpu.make_async_copy(
            cache.at[:, pl.ds(base, rows)], window.at[i], arrived.at[i]
        )
        copy.start()
        begins.append(begin)
        bases.append(base)
        copies.append(copy)
        begin = begin + lengths[i]
    for i in range(requests):
        copies[i].wait()
        scores = lax.dot_general(
            queries[i], window[i], (((0,), (0,)), ((), ())), preferred_element_type=F32
        ) * scale
        place = bases[i] + lax.broadcasted_iota(jnp.int32, scores.shape, 1)
        live = (place >= begins[i]) & (place < begins[i] + lengths[i])
        scores = jnp.where(live, scores, -1e30)
        largest = jnp.max(scores, 1, keepdims=True)
        weights = jnp.where(live, jnp.exp(scores - largest), 0.0)
        totals = jnp.sum(weights, 1, keepdims=True)
        weighted = lax.dot_general(
            weights.astype(BF), window[i, :LAT, :], (((1,), (1,)), ((), ())),
            preferred_element_type=F32,
        )
        latent[i] = (weighted / totals).astype(BF)


def attend(lengths, queries, cache):
    requests, heads, width = queries.shape
    rows = LONGEST + ALIGN
    vmem = pl.BlockSpec(memory_space=pltpu.VMEM)
    return pl.pallas_call(
        attend_kernel,
        out_shape=jax.ShapeDtypeStruct((requests, heads, LAT), BF),
        in_specs=[
            pl.BlockSpec(memory_space=pltpu.SMEM), vmem, pl.BlockSpec(memory_space=pl.ANY),
        ],
        out_specs=vmem,
        scratch_shapes=[
            pltpu.VMEM((requests, width, rows), BF),
            pltpu.SemaphoreType.DMA((requests,)),
        ],
        compiler_params=pltpu.CompilerParams(vmem_limit_bytes=40 * 2**20),
        name="attend",
    )(lengths, queries.swapaxes(1, 2), cache.T)


def expert_kernel(steps, place, *refs):
    own, pair, extra = refs[0:N], refs[N : 2 * N], refs[2 * N : 3 * N]
    gate_own, gate_pair, up_own, up_pair, hidden, own_sum, pair_sum = refs[3 * N :]
    step = pl.program_id(0)

    @pl.when(step == 0)
    def _():
        own_sum[...] = jnp.zeros_like(own_sum)
        pair_sum[...] = jnp.zeros_like(pair_sum)

    def product(chunks, gate, up):
        rows = jnp.concatenate([chunk[...] for chunk in chunks], 0)
        weights = jnp.concatenate([gate[...], up[...]], 1)
        return jnp.dot(rows, weights, preferred_element_type=F32)

    own_sum[...] += product(own, gate_own, up_own)
    pair_sum[...] += product(pair, gate_pair, up_pair)

    @pl.when(step == steps - 1)
    def _():
        units = hidden.shape[1]
        rows = hidden.shape[0] // (N * N)
        for i in range(N):
            pieces = extra[i][...].astype(F32)
            lane = lax.broadcasted_iota(jnp.int32, pieces.shape, 1) & (EXPERTS - 1)
            mix = jnp.sum(jnp.where(lane == place[1], pieces, 0.0), 1, keepdims=True)
            for j in range(N):
                here = pl.ds((i * N + j) * rows, rows)
                there = pl.ds((j * N + i) * rows, rows)
                both = own_sum[here, :] + pair_sum[there, :]
                gate, up = both[:, :units], both[:, units:]
                acted = gate / (1.0 + jnp.exp(-gate)) * up * mix[j * rows : (j + 1) * rows]
                hidden[here, :] = acted.astype(BF)


def expert_hidden(place, own, pair, w_gate, w_up):
    depth, units = w_gate.shape
    wide = depth // 2
    block = 512
    steps = wide // block
    rows = own[0].shape[0]
    chunk = pl.BlockSpec((rows, block), lambda k, p: (0, k))
    extra = pl.BlockSpec((rows, EXTRA), lambda k, p: (0, wide // EXTRA))
    mine = pl.BlockSpec((block, units), lambda k, p: (p[0] * steps + k, 0))
    theirs = pl.BlockSpec((block, units), lambda k, p: ((1 - p[0]) * steps + k, 0))
    return pl.pallas_call(
        functools.partial(expert_kernel, steps),
        out_shape=[
            jax.ShapeDtypeStruct((N * rows, units), BF),
            jax.ShapeDtypeStruct((N * rows, 2 * units), F32),
            jax.ShapeDtypeStruct((N * rows, 2 * units), F32),
        ],
        grid_spec=pltpu.PrefetchScalarGridSpec(
            num_scalar_prefetch=1,
            grid=(steps,),
            in_specs=[chunk] * (2 * N) + [extra] * N + [mine, theirs, mine, theirs],
            out_specs=[
                pl.BlockSpec((N * rows, units), lambda k, p: (0, 0)),
                pl.BlockSpec((N * rows, 2 * units), lambda k, p: (0, 0)),
                pl.BlockSpec((N * rows, 2 * units), lambda k, p: (0, 0)),
            ],
        ),
        compiler_params=pltpu.CompilerParams(vmem_limit_bytes=40 * 2**20),
        name="expert_hidden",
    )(place, *own, *pair, *own, w_gate, w_gate, w_up, w_up)[0]


def plane_index(y, x, c):
    return (y % N * N + x % N) * 2 + c


def leading(block, offset):
    pairs = [
        (plane_index(y, x, c), plane_index(y + offset * (1 - c), x + offset * c, c))
        for y in range(N) for x in range(N) for c in range(2)
    ]
    return lax.ppermute(block, PLANE, pairs)


def trailing(block, offset):
    pairs = [
        (plane_index(y, x, c), plane_index(y + offset * c, x + offset * (1 - c), c))
        for y in range(N) for x in range(N) for c in range(2)
    ]
    return lax.ppermute(block, PLANE, pairs)


def upright(block, offset):
    return lax.ppermute(block, "z", [(i, (i + offset) % N) for i in range(N)])


def swap(block):
    return lax.ppermute(block, "c", [(0, 1), (1, 0)])


def rolled(block, shift, dim):
    return lax.dynamic_slice_in_dim(
        jnp.concatenate([block, block], dim), shift, block.shape[dim], dim
    )


def half(block, which, dim):
    size = block.shape[dim] // 2
    return lax.dynamic_slice_in_dim(block, which * size, size, dim)


def mm(a, b):
    return jnp.dot(a, b, preferred_element_type=F32)


def scatter_axis(chunks, send):
    arrived = [send(chunks[k], k) for k in range(1, N)]
    total = chunks[0].astype(F32)
    for block in arrived:
        total = total + block.astype(F32)
    return total


def gather_axis(block, send):
    return [block] + [send(block, -k) for k in range(1, N)]


def local(
    hidden_in, queries, cache, lengths, value_up, out_proj, norm_gain, routes, route_weight,
    w_gate, w_up, w_down,
):
    zi, yi, xi, ci = (lax.axis_index(a) for a in AXES)
    other = 1 - ci
    width = hidden_in.shape[1]
    wide = width // 2
    requests = hidden_in.shape[0]
    chip = 2 * requests

    def chip_rows(mine, theirs):
        return jnp.concatenate(
            [jnp.where(ci == 0, mine, theirs), jnp.where(ci == 0, theirs, mine)], 0
        )

    chip_hidden = chip_rows(half(hidden_in, ci, 1), swap(half(hidden_in, other, 1)))
    gain = lax.dynamic_slice_in_dim(norm_gain, ci * wide, wide, 0)

    experts = jnp.arange(EXPERTS, dtype=jnp.int32)
    dense = jnp.sum(
        jnp.where(routes[:, :, None] == experts, route_weight[:, :, None], 0.0), 1
    )
    top = lax.reduce_precision(dense, 8, 7)
    middle = lax.reduce_precision(dense - top, 8, 7)
    pieces = [top, middle, dense - top - middle, jnp.zeros_like(dense)]
    pieces = jnp.concatenate(pieces, 1).astype(BF)
    chip_pieces = chip_rows(pieces, swap(pieces))

    down_other = swap(half(w_down[0], other, 1))
    down_pair = jnp.concatenate([half(w_down[0], ci, 1), down_other], 0)

    latent = attend(lengths, queries, cache)
    regrouped = lax.all_to_all(latent, PLANE, split_axis=1, concat_axis=0, tiled=True)
    head_out = jnp.einsum("thl,hlv->thv", regrouped, value_up, preferred_element_type=F32)
    head_out = head_out.astype(BF).reshape(N, N, chip, -1)
    head_out = rolled(rolled(head_out, yi, 0), xi, 1)
    flipped = head_out.swapaxes(0, 1)
    own_order = jnp.where(ci == 0, head_out, flipped).reshape(N * N * chip, -1)
    pair_order = jnp.where(ci == 0, flipped, head_out).reshape(N * N * chip, -1)
    sent = swap(mm(pair_order, half(out_proj, other, 1)).astype(BF))
    partial = mm(own_order, half(out_proj, ci, 1)) + sent.astype(F32)
    partial = partial.astype(BF).reshape(N, N * chip, wide)
    partial = scatter_axis([partial[k] for k in range(N)], leading)
    partial = partial.astype(BF).reshape(N, chip, wide)
    attended = scatter_axis([partial[k] for k in range(N)], trailing)
    residual = chip_hidden.astype(F32) + attended
    squares = jnp.sum(residual * residual, 1, keepdims=True)
    squares = squares + swap(squares)
    normed = (residual * lax.rsqrt(squares / width + 1e-06) * gain).astype(BF)

    shard = jnp.concatenate([normed, chip_pieces], 1)
    shard = jnp.concatenate(gather_axis(shard, upright), 0)
    shard = jnp.concatenate(gather_axis(shard, trailing), 0)
    own = gather_axis(shard, leading)
    pair = [swap(chunk) for chunk in own]

    place = jnp.stack([ci, plane_index(yi, xi, ci)]).astype(jnp.int32)
    hidden = expert_hidden(place, own, pair, w_gate[0], w_up[0])
    theirs = swap(hidden).reshape(N, N, N * chip, -1).swapaxes(0, 1).reshape(hidden.shape)
    both = jnp.concatenate([hidden, theirs], 1).reshape(N, N * N * chip, -1)
    out = scatter_axis([mm(both[k], down_pair).astype(BF) for k in range(N)], leading)
    out = out.astype(BF).reshape(N, N * chip, wide)
    out = scatter_axis([out[k] for k in range(N)], trailing)
    out = out.astype(BF).reshape(N, chip, wide)
    routed = scatter_axis([out[k] for k in range(N)], upright)
    layer_out = (residual + routed).astype(BF).reshape(2, requests, wide)
    mine = lax.dynamic_index_in_dim(layer_out, ci, 0, keepdims=False)
    theirs = swap(lax.dynamic_index_in_dim(layer_out, other, 0, keepdims=False))
    left = jnp.where(ci == 0, mine, theirs)
    right = jnp.where(ci == 0, theirs, mine)
    return jnp.concatenate([left, right], 1)


def solution(mesh):
    torus = Mesh(mesh.devices.reshape(N, N, N, 2), AXES)
    in_specs = (
        P(AXES, None),
        P(AXES, None, None),
        P(AXES, None),
        P(AXES),
        P(PLANE, None, None),
        P(PLANE, None),
        P(),
        P(AXES, None),
        P(AXES, None),
        P(PLANE, None, "z"),
        P(PLANE, None, "z"),
        P(PLANE, "z", None),
    )
    return jax.shard_map(
        local, mesh=torus, in_specs=in_specs, out_specs=P(AXES, None), check_vma=False
    )
```

```python
import functools

import jax
import jax.numpy as jnp
from jax import lax
from jax.experimental import pallas as pl
from jax.experimental.pallas import tpu as pltpu
from jax.sharding import Mesh, PartitionSpec as P

LAT = 512
ROPE = 64
DV = 128
LONGEST = 1024
ALIGN = 128
N = 4
EXPERTS = 32
EXTRA = 128
AXES = ("z", "y", "x", "c")
PLANE = ("y", "x", "c")
BF = jnp.bfloat16
F32 = jnp.float32


def attend_kernel(
    core, lengths, queries, cache, w_gate, w_up, w_down,
    latent, gate_out, up_out, down_out, window, gate_buf, up_buf, down_buf, arrived, staged,
):
    requests = queries.shape[0]
    rows = window.shape[2]
    scale = (DV + ROPE) ** (-0.5)
    begins, bases, copies = [], [], []
    begin = jnp.int32(0)
    for i in range(requests):
        base = jnp.minimum(begin // ALIGN * ALIGN, cache.shape[1] - rows)
        base = pl.multiple_of(base, ALIGN)
        copy = pltpu.make_async_copy(
            cache.at[:, pl.ds(base, rows)], window.at[i], arrived.at[i]
        )
        copy.start()
        begins.append(begin)
        bases.append(base)
        copies.append(copy)
        begin = begin + lengths[i]
    size = gate_out.shape[0]
    offset = pl.multiple_of((1 - core[0]) * size, 512)
    loads = [
        pltpu.make_async_copy(w_gate.at[pl.ds(offset, size), :], gate_buf, staged.at[0]),
        pltpu.make_async_copy(w_up.at[pl.ds(offset, size), :], up_buf, staged.at[1]),
        pltpu.make_async_copy(w_down.at[:, pl.ds(offset, size)], down_buf, staged.at[2]),
    ]
    stores = [
        pltpu.make_async_copy(gate_buf, gate_out, staged.at[3]),
        pltpu.make_async_copy(up_buf, up_out, staged.at[4]),
        pltpu.make_async_copy(down_buf, down_out, staged.at[5]),
    ]
    for load in loads:
        load.start()
    for i in range(requests):
        if i == requests // 2:
            for load, store in zip(loads, stores):
                load.wait()
                store.start()
        copies[i].wait()
        scores = lax.dot_general(
            queries[i], window[i], (((0,), (0,)), ((), ())), preferred_element_type=F32
        ) * scale
        place = bases[i] + lax.broadcasted_iota(jnp.int32, scores.shape, 1)
        live = (place >= begins[i]) & (place < begins[i] + lengths[i])
        scores = jnp.where(live, scores, -1e30)
        largest = jnp.max(scores, 1, keepdims=True)
        weights = jnp.where(live, jnp.exp(scores - largest), 0.0)
        totals = jnp.sum(weights, 1, keepdims=True)
        weighted = lax.dot_general(
            weights.astype(BF), window[i, :LAT, :], (((1,), (1,)), ((), ())),
            preferred_element_type=F32,
        )
        latent[i] = (weighted / totals).astype(BF)
    for store in stores:
        store.wait()


def attend(core, lengths, queries, cache, w_gate, w_up, w_down):
    requests, heads, width = queries.shape
    rows = LONGEST + ALIGN
    depth, units = w_gate.shape
    vmem = pl.BlockSpec(memory_space=pltpu.VMEM)
    smem = pl.BlockSpec(memory_space=pltpu.SMEM)
    hbm = pl.BlockSpec(memory_space=pl.ANY)
    return pl.pallas_call(
        attend_kernel,
        out_shape=[
            jax.ShapeDtypeStruct((requests, heads, LAT), BF),
            jax.ShapeDtypeStruct((depth // 2, units), BF),
            jax.ShapeDtypeStruct((depth // 2, units), BF),
            jax.ShapeDtypeStruct((units, depth // 2), BF),
        ],
        in_specs=[smem, smem, vmem, hbm, hbm, hbm, hbm],
        out_specs=[vmem, hbm, hbm, hbm],
        scratch_shapes=[
            pltpu.VMEM((requests, width, rows), BF),
            pltpu.VMEM((depth // 2, units), BF),
            pltpu.VMEM((depth // 2, units), BF),
            pltpu.VMEM((units, depth // 2), BF),
            pltpu.SemaphoreType.DMA((requests,)),
            pltpu.SemaphoreType.DMA((6,)),
        ],
        compiler_params=pltpu.CompilerParams(vmem_limit_bytes=56 * 2**20),
        name="attend",
    )(core, lengths, queries.swapaxes(1, 2), cache.T, w_gate, w_up, w_down)


def product_kernel(count, core, *refs):
    chunks, weights = refs[:count], refs[count : count + 4]
    own_sum, cross_sum, held, arrived = refs[count + 4 :]
    wide, units = held.shape[1:]
    offset = pl.multiple_of(core[0] * wide, 512)
    copies = []
    for i, weight in enumerate(weights):
        source = weight.at[pl.ds(offset, wide), :] if i < 2 else weight
        copies.append(pltpu.make_async_copy(source, held.at[i], arrived.at[i]))
        copies[i].start()
    pieces = jnp.concatenate([chunk[:, wide:] for chunk in chunks], 0).astype(F32)
    lane = lax.broadcasted_iota(jnp.int32, pieces.shape, 1)
    squares = jnp.sum(jnp.where(lane >= 3 * EXPERTS, pieces, 0.0), 1, keepdims=True)
    cross_sum[:, 2 * units :] = jnp.broadcast_to(squares, pieces.shape)
    rows = jnp.concatenate([chunk[:, :wide] for chunk in chunks], 0)
    for i in range(4):
        copies[i].wait()
        total = own_sum if i < 2 else cross_sum
        total[:, i % 2 * units : (i % 2 + 1) * units] = jnp.dot(
            rows, held[i], preferred_element_type=F32
        )


def expert_products(core, chunks, w_gate, w_up, gate_other, up_other):
    depth, units = w_gate.shape
    wide = depth // 2
    rows = sum(chunk.shape[0] for chunk in chunks)
    vmem = pl.BlockSpec(memory_space=pltpu.VMEM)
    hbm = pl.BlockSpec(memory_space=pl.ANY)
    return pl.pallas_call(
        functools.partial(product_kernel, len(chunks)),
        out_shape=[
            jax.ShapeDtypeStruct((rows, 2 * units), F32),
            jax.ShapeDtypeStruct((rows, 2 * units + EXTRA), F32),
        ],
        in_specs=[pl.BlockSpec(memory_space=pltpu.SMEM)] + [vmem] * len(chunks) + [hbm] * 4,
        out_specs=[vmem, vmem],
        scratch_shapes=[
            pltpu.VMEM((4, wide, units), BF),
            pltpu.SemaphoreType.DMA((4,)),
        ],
        compiler_params=pltpu.CompilerParams(vmem_limit_bytes=48 * 2**20),
        cost_estimate=pl.CostEstimate(
            flops=4 * rows * depth * units, bytes_accessed=4 * depth * units, transcendentals=0
        ),
        name="expert_products",
    )(core, *chunks, w_gate, w_up, gate_other, up_other)


def finish_kernel(width, rank, *refs):
    own_sums, refs = refs[:N], refs[N:]
    pair_sums, refs = refs[:N], refs[N:]
    extras, hidden, flipped = refs[:-2], refs[-2], refs[-1]
    units = hidden.shape[1]
    rows = hidden.shape[0] // (N * N)
    for i in range(N):
        pieces = jnp.concatenate([extras[2 * i][...], extras[2 * i + 1][...]], 0).astype(F32)
        lane = lax.broadcasted_iota(jnp.int32, pieces.shape, 1)
        weighs = (lane < 3 * EXPERTS) & ((lane & (EXPERTS - 1)) == rank[0])
        mix = jnp.sum(jnp.where(weighs, pieces, 0.0), 1, keepdims=True)
        squares = jnp.sum(jnp.where(lane >= 3 * EXPERTS, pieces, 0.0), 1, keepdims=True)
        for j in range(N):
            here, there = slice(j * rows, (j + 1) * rows), slice(i * rows, (i + 1) * rows)
            pair = pair_sums[j][there, :]
            square = squares[here] + pair[:, 2 * units : 2 * units + 1]
            factor = lax.rsqrt(square / width + 1e-06)
            both = (own_sums[i][here, :] + pair[:, : 2 * units]) * factor
            gate, up = both[:, :units], both[:, units:]
            acted = (gate / (1.0 + jnp.exp(-gate)) * up * mix[here]).astype(BF)
            hidden[(i * N + j) * rows : (i * N + j + 1) * rows, :] = acted
            flipped[(j * N + i) * rows : (j * N + i + 1) * rows, :] = acted


def expert_finish(rank, width, own_sums, pair_sums, pieces):
    rows = pieces[0][0].shape[0] * 2
    units = own_sums[0][0].shape[1] // 2
    wide = width // 2

    def sums_spec(item):
        index = item[1] // rows
        return pl.BlockSpec((rows, item[0].shape[1]), lambda k, r: (index, 0))

    extra = pl.BlockSpec((rows // 2, EXTRA), lambda k, r: (0, wide // EXTRA))
    whole = pl.BlockSpec((N * rows, units), lambda k, r: (0, 0))
    parts = [part for chunk in pieces for part in chunk]
    sums = list(own_sums) + list(pair_sums)
    return pl.pallas_call(
        functools.partial(finish_kernel, width),
        out_shape=[jax.ShapeDtypeStruct((N * rows, units), BF)] * 2,
        grid_spec=pltpu.PrefetchScalarGridSpec(
            num_scalar_prefetch=1,
            grid=(1,),
            in_specs=[sums_spec(item) for item in sums] + [extra] * len(parts),
            out_specs=[whole, whole],
        ),
        compiler_params=pltpu.CompilerParams(vmem_limit_bytes=32 * 2**20),
        name="expert_finish",
    )(rank, *[item[0] for item in sums], *parts)


def plane_index(y, x, c):
    return (y % N * N + x % N) * 2 + c


def leading(block, offset):
    pairs = [
        (plane_index(y, x, c), plane_index(y + offset * (1 - c), x + offset * c, c))
        for y in range(N) for x in range(N) for c in range(2)
    ]
    return lax.ppermute(block, PLANE, pairs)


def trailing(block, offset):
    pairs = [
        (plane_index(y, x, c), plane_index(y + offset * c, x + offset * (1 - c), c))
        for y in range(N) for x in range(N) for c in range(2)
    ]
    return lax.ppermute(block, PLANE, pairs)


def upright(block, offset):
    return lax.ppermute(block, "z", [(i, (i + offset) % N) for i in range(N)])


def swap(block):
    return lax.ppermute(block, "c", [(0, 1), (1, 0)])


def rolled(block, shift, dim):
    return lax.dynamic_slice_in_dim(
        jnp.concatenate([block, block], dim), shift, block.shape[dim], dim
    )


def half(block, which, dim):
    size = block.shape[dim] // 2
    return lax.dynamic_slice_in_dim(block, which * size, size, dim)


def mm(a, b):
    return jnp.dot(a, b, preferred_element_type=F32)


def three_pieces(values):
    top = lax.reduce_precision(values, 8, 7)
    middle = lax.reduce_precision(values - top, 8, 7)
    return [top, middle, values - top - middle]


def scatter_axis(chunks, send):
    arrived = [send(chunks[k], k) for k in range(1, N)]
    total = chunks[0].astype(F32)
    for block in arrived:
        total = total + block.astype(F32)
    return total


def gather_axis(block, send):
    return [block] + [send(block, -k) for k in range(1, N)]


def local(
    hidden_in, queries, cache, lengths, value_up, out_proj, norm_gain, routes, route_weight,
    w_gate, w_up, w_down,
):
    zi, yi, xi, ci = (lax.axis_index(a) for a in AXES)
    other = 1 - ci
    width = hidden_in.shape[1]
    wide = width // 2
    part = wide // 2
    requests = hidden_in.shape[0]
    chip = 2 * requests

    def chip_rows(mine, theirs):
        return jnp.concatenate(
            [jnp.where(ci == 0, mine, theirs), jnp.where(ci == 0, theirs, mine)], 0
        )

    chip_hidden = chip_rows(half(hidden_in, ci, 1), swap(half(hidden_in, other, 1)))
    gain = lax.dynamic_slice_in_dim(norm_gain, ci * wide, wide, 0)

    experts = jnp.arange(EXPERTS, dtype=jnp.int32)
    dense = jnp.sum(
        jnp.where(routes[:, :, None] == experts, route_weight[:, :, None], 0.0), 1
    )
    pieces = jnp.concatenate(three_pieces(dense) + [jnp.zeros_like(dense)], 1).astype(BF)
    chip_pieces = chip_rows(pieces, swap(pieces))

    core = ci.astype(jnp.int32).reshape(1)
    latent, *sent = attend(core, lengths, queries, cache, w_gate[0], w_up[0], w_down[0])
    gate_other, up_other, down_other = (swap(block) for block in sent)
    regrouped = lax.all_to_all(latent, PLANE, split_axis=1, concat_axis=0, tiled=True)
    regrouped, gate_other, up_other, down_other = lax.optimization_barrier(
        (regrouped, gate_other, up_other, down_other)
    )
    down_own = half(w_down[0], ci, 1)
    down_a = jnp.concatenate([down_own[:, :part], down_other[:, :part]], 0)
    down_b = jnp.concatenate([down_own[:, part:], down_other[:, part:]], 0)
    head_out = jnp.einsum("thl,hlv->thv", regrouped, value_up, preferred_element_type=F32)
    head_out = head_out.astype(BF).reshape(N, N, chip, -1)
    head_out = rolled(rolled(head_out, yi, 0), xi, 1)
    flipped = head_out.swapaxes(0, 1)
    own_order = jnp.where(ci == 0, head_out, flipped).reshape(N * N * chip, -1)
    pair_order = jnp.where(ci == 0, flipped, head_out).reshape(N * N * chip, -1)
    sent = swap(mm(pair_order, half(out_proj, other, 1)).astype(BF))
    partial = lax.optimization_barrier(mm(own_order, half(out_proj, ci, 1)))
    partial = partial + sent.astype(F32)
    partial = partial.astype(BF).reshape(N, N * chip, wide)
    partial = scatter_axis([partial[k] for k in range(N)], leading)
    partial = partial.astype(BF).reshape(N, chip, wide)
    attended = scatter_axis([partial[k] for k in range(N)], trailing)
    residual = chip_hidden.astype(F32) + attended
    squares = jnp.sum(residual * residual, 1, keepdims=True)
    lane = jnp.arange(EXTRA, dtype=jnp.int32)
    extra = chip_pieces
    for place, piece in enumerate(three_pieces(squares)):
        extra = jnp.where(lane == 3 * EXPERTS + place, piece.astype(BF), extra)

    shard = jnp.concatenate([(residual * gain).astype(BF), extra], 1)
    shard = jnp.concatenate(gather_axis(shard, upright), 0)
    blocks = gather_axis(shard, trailing)
    near_a = jnp.concatenate(blocks[: N // 2], 0)
    near_b = jnp.concatenate(blocks[N // 2 :], 0)
    before_a, after_b = leading(near_a, 1), leading(near_b, -1)
    before_b, after_a = leading(near_b, 1), leading(near_a, -1)

    def products(chunks):
        own, cross = expert_products(core, chunks, w_gate[0], w_up[0], gate_other, up_other)
        return own, swap(cross)

    sums_0 = products([near_a, near_b])
    before_a, after_b, _ = lax.optimization_barrier((before_a, after_b, sums_0[0]))
    far_a, far_b = leading(before_a, 1), leading(after_b, -1)
    sums_13 = products([after_a, after_b, before_a, before_b])
    sums_2 = products([far_a, far_b])
    own_sums, pair_sums = (
        [(sums_0[p], 0), (sums_13[p], 0), (sums_2[p], 0), (sums_13[p], near_a.shape[0] * 2)]
        for p in range(2)
    )
    hidden, flipped = expert_finish(
        plane_index(yi, xi, ci).astype(jnp.int32).reshape(1), width, own_sums, pair_sums,
        [[near_a, near_b], [after_a, after_b], [far_a, far_b], [before_a, before_b]],
    )
    theirs = swap(flipped)
    both = jnp.concatenate([hidden, theirs], 1).reshape(N, N * N * chip, -1)

    first = lax.optimization_barrier((
        mm(both[2], down_a).astype(BF), mm(both[2], down_b).astype(BF),
        mm(both[1], down_b).astype(BF), mm(both[3], down_a).astype(BF),
    ))
    relay_a, relay_b = leading(first[0], 1), leading(first[1], -1)
    next_b, last_a = leading(first[2], 1), leading(first[3], -1)
    next_a = leading((mm(both[1], down_a) + relay_a.astype(F32)).astype(BF), 1)
    last_b = leading((mm(both[3], down_b) + relay_b.astype(F32)).astype(BF), -1)
    out_a = mm(both[0], down_a) + last_a.astype(F32) + next_a.astype(F32)
    out_b = mm(both[0], down_b) + next_b.astype(F32) + last_b.astype(F32)
    out = jnp.concatenate([out_a.astype(BF), out_b.astype(BF)], 1).reshape(N, N * chip, wide)
    out = scatter_axis([out[k] for k in range(N)], trailing)
    out = out.astype(BF).reshape(N, chip, wide)
    routed = scatter_axis([out[k] for k in range(N)], upright)
    layer_out = (residual + routed).astype(BF).reshape(2, requests, wide)
    mine = lax.dynamic_index_in_dim(layer_out, ci, 0, keepdims=False)
    theirs = swap(lax.dynamic_index_in_dim(layer_out, other, 0, keepdims=False))
    left = jnp.where(ci == 0, mine, theirs)
    right = jnp.where(ci == 0, theirs, mine)
    return jnp.concatenate([left, right], 1)


def solution(mesh):
    torus = Mesh(mesh.devices.reshape(N, N, N, 2), AXES)
    in_specs = (
        P(AXES, None),
        P(AXES, None, None),
        P(AXES, None),
        P(AXES),
        P(PLANE, None, None),
        P(PLANE, None),
        P(),
        P(AXES, None),
        P(AXES, None),
        P(PLANE, None, "z"),
        P(PLANE, None, "z"),
        P(PLANE, "z", None),
    )
    return jax.shard_map(
        local, mesh=torus, in_specs=in_specs, out_specs=P(AXES, None), check_vma=False
    )
```

```python
import functools

import jax
import jax.numpy as jnp
from jax import lax
from jax.experimental import pallas as pl
from jax.experimental.pallas import tpu as pltpu
from jax.sharding import Mesh, PartitionSpec as P

LAT = 512
ROPE = 64
DV = 128
LONGEST = 1024
ALIGN = 128
PIECES = 4
N = 4
EXPERTS = 32
EXTRA = 128
AXES = ("z", "y", "x", "c")
PLANE = ("y", "x", "c")
BF = jnp.bfloat16
F32 = jnp.float32


def attend_kernel(lengths, queries, cache, latent, window, arrived):
    requests = queries.shape[0]
    rows = window.shape[2]
    piece = window.shape[1] // PIECES
    scale = (DV + ROPE) ** (-0.5)
    begins, bases, copies = [], [], []
    begin = jnp.int32(0)
    for i in range(requests):
        base = jnp.minimum(begin // ALIGN * ALIGN, cache.shape[1] - rows)
        base = pl.multiple_of(base, ALIGN)
        copies.append([
            pltpu.make_async_copy(
                cache.at[pl.ds(j * piece, piece), pl.ds(base, rows)],
                window.at[i, pl.ds(j * piece, piece), :],
                arrived.at[i, j],
            )
            for j in range(PIECES)
        ])
        begins.append(begin)
        bases.append(base)
        begin = begin + lengths[i]
    for copy in copies[0] + copies[1]:
        copy.start()
    for i in range(requests):
        for copy in copies[i]:
            copy.wait()
        if i + 2 < requests:
            for copy in copies[i + 2]:
                copy.start()
        scores = lax.dot_general(
            queries[i], window[i], (((0,), (0,)), ((), ())), preferred_element_type=F32
        ) * scale
        place = bases[i] + lax.broadcasted_iota(jnp.int32, scores.shape, 1)
        live = (place >= begins[i]) & (place < begins[i] + lengths[i])
        scores = jnp.where(live, scores, -1e30)
        largest = jnp.max(scores, 1, keepdims=True)
        weights = jnp.where(live, jnp.exp(scores - largest), 0.0)
        totals = jnp.sum(weights, 1, keepdims=True)
        weighted = lax.dot_general(
            weights.astype(BF), window[i, :LAT, :], (((1,), (1,)), ((), ())),
            preferred_element_type=F32,
        )
        latent[i] = (weighted / totals).astype(BF)


def attend(lengths, queries, cache):
    requests, heads, width = queries.shape
    rows = LONGEST + ALIGN
    vmem = pl.BlockSpec(memory_space=pltpu.VMEM)
    return pl.pallas_call(
        attend_kernel,
        out_shape=jax.ShapeDtypeStruct((requests, heads, LAT), BF),
        in_specs=[
            pl.BlockSpec(memory_space=pltpu.SMEM), vmem, pl.BlockSpec(memory_space=pl.ANY),
        ],
        out_specs=vmem,
        scratch_shapes=[
            pltpu.VMEM((requests, width, rows), BF),
            pltpu.SemaphoreType.DMA((requests, PIECES)),
        ],
        compiler_params=pltpu.CompilerParams(vmem_limit_bytes=56 * 2**20),
        name="attend",
    )(lengths, queries.swapaxes(1, 2), cache.T)


def project_kernel(rows, weight, result):
    block = 512
    for k in range(result.shape[1] // block):
        here = slice(k * block, (k + 1) * block)
        product = jnp.dot(rows[...], weight[:, here], preferred_element_type=F32)
        result[:, here] = product.astype(result.dtype)


def project(rows, weight, dtype):
    count, depth = rows.shape
    wide = weight.shape[1]
    vmem = pl.BlockSpec(memory_space=pltpu.VMEM)
    return pl.pallas_call(
        project_kernel,
        out_shape=jax.ShapeDtypeStruct((count, wide), dtype),
        in_specs=[vmem, vmem],
        out_specs=vmem,
        compiler_params=pltpu.CompilerParams(vmem_limit_bytes=16 * 2**20),
        cost_estimate=pl.CostEstimate(
            flops=2 * count * depth * wide, bytes_accessed=2 * depth * wide, transcendentals=0
        ),
        name="project",
    )(rows, weight)


def down_kernel(picks, core, hidden, theirs, weight, other, *results):
    rows, part = results[0].shape

    def run(side):
        for (chunk, k), result in zip(picks, results):
            here = slice(chunk * rows, (chunk + 1) * rows)
            mine = slice((2 * side + k) * part, (2 * side + k + 1) * part)
            product = jnp.dot(
                theirs[here, :], other[:, k * part : (k + 1) * part], preferred_element_type=F32
            )
            product += jnp.dot(hidden[here, :], weight[:, mine], preferred_element_type=F32)
            result[...] = product.astype(result.dtype)

    for side in range(2):
        pl.when(core[0] == side)(functools.partial(run, side))


def down_products(picks, dtype, core, hidden, theirs, weight, other):
    rows, units = hidden.shape[0] // N, hidden.shape[1]
    part = other.shape[1] // 2
    vmem = pl.BlockSpec(memory_space=pltpu.VMEM)
    return pl.pallas_call(
        functools.partial(down_kernel, picks),
        out_shape=[jax.ShapeDtypeStruct((rows, part), dtype)] * len(picks),
        in_specs=[pl.BlockSpec(memory_space=pltpu.SMEM)] + [vmem] * 4,
        out_specs=[vmem] * len(picks),
        compiler_params=pltpu.CompilerParams(vmem_limit_bytes=16 * 2**20),
        cost_estimate=pl.CostEstimate(
            flops=4 * len(picks) * rows * part * units,
            bytes_accessed=2 * len(picks) * rows * part, transcendentals=0,
        ),
        name="down",
    )(core, hidden, theirs, weight, other)


def product_kernel(count, place, *refs):
    chunks, (gate, up, gate_other, up_other) = refs[:count], refs[count : count + 4]
    own_sum, cross_sum = refs[count + 4 :]
    wide, units = gate_other.shape

    def columns(begin, size):
        return jnp.concatenate([chunk[:, begin : begin + size] for chunk in chunks], 0)

    pieces = columns(wide, EXTRA).astype(F32)
    lane = lax.broadcasted_iota(jnp.int32, pieces.shape, 1)
    weighs = (lane < 3 * EXPERTS) & ((lane & (EXPERTS - 1)) == place[1])
    mix = jnp.sum(jnp.where(weighs, pieces, 0.0), 1, keepdims=True)
    squares = jnp.sum(jnp.where(lane >= 3 * EXPERTS, pieces, 0.0), 1, keepdims=True)
    own_sum[:, 2 * units :] = jnp.where(lane == 0, squares, mix)
    cross_sum[:, 2 * units :] = jnp.broadcast_to(squares, pieces.shape)
    block = 512
    for k in range(wide // block):
        here = pl.ds(k * block, block)
        mine = pl.ds(pl.multiple_of(place[0] * wide + k * block, block), block)
        tokens = columns(k * block, block)
        own = jnp.concatenate([gate[mine, :], up[mine, :]], 1)
        cross = jnp.concatenate([gate_other[here, :], up_other[here, :]], 1)
        for total, weights in ((own_sum, own), (cross_sum, cross)):
            product = jnp.dot(tokens, weights, preferred_element_type=F32)
            if k == 0:
                total[:, : 2 * units] = product
            else:
                total[:, : 2 * units] += product


def expert_products(place, chunks, w_gate, w_up, gate_other, up_other):
    depth, units = w_gate.shape
    rows = sum(chunk.shape[0] for chunk in chunks)
    vmem = pl.BlockSpec(memory_space=pltpu.VMEM)
    return pl.pallas_call(
        functools.partial(product_kernel, len(chunks)),
        out_shape=[jax.ShapeDtypeStruct((rows, 2 * units + EXTRA), F32)] * 2,
        in_specs=[pl.BlockSpec(memory_space=pltpu.SMEM)] + [vmem] * (len(chunks) + 4),
        out_specs=[vmem, vmem],
        compiler_params=pltpu.CompilerParams(vmem_limit_bytes=16 * 2**20),
        cost_estimate=pl.CostEstimate(
            flops=4 * rows * depth * units, bytes_accessed=4 * depth * units, transcendentals=0
        ),
        name="expert_products",
    )(place, *chunks, w_gate, w_up, gate_other, up_other)


def finish_kernel(width, *refs):
    own_sums, pair_sums, (hidden, flipped) = refs[:N], refs[N : 2 * N], refs[2 * N :]
    units = hidden.shape[1]
    rows = hidden.shape[0] // (N * N)
    for i in range(N):
        for j in range(N):
            own = own_sums[i][j * rows : (j + 1) * rows, :]
            pair = pair_sums[j][i * rows : (i + 1) * rows, :]
            square = own[:, 2 * units : 2 * units + 1] + pair[:, 2 * units : 2 * units + 1]
            mix = own[:, 2 * units + 1 : 2 * units + 2]
            factor = lax.rsqrt(square / width + 1e-06)
            both = (own[:, : 2 * units] + pair[:, : 2 * units]) * factor
            gate, up = both[:, :units], both[:, units:]
            acted = (gate / (1.0 + jnp.exp(-gate)) * up * mix).astype(BF)
            hidden[(i * N + j) * rows : (i * N + j + 1) * rows, :] = acted
            flipped[(j * N + i) * rows : (j * N + i + 1) * rows, :] = acted


def expert_finish(width, rows, own_sums, pair_sums):
    columns = own_sums[0][0].shape[1]
    units = (columns - EXTRA) // 2

    def sums_spec(item):
        index = item[1] // rows
        return pl.BlockSpec((rows, columns), lambda k: (index, 0))

    whole = pl.BlockSpec((N * rows, units), lambda k: (0, 0))
    sums = list(own_sums) + list(pair_sums)
    return pl.pallas_call(
        functools.partial(finish_kernel, width),
        out_shape=[jax.ShapeDtypeStruct((N * rows, units), BF)] * 2,
        grid=(1,),
        in_specs=[sums_spec(item) for item in sums],
        out_specs=[whole, whole],
        compiler_params=pltpu.CompilerParams(vmem_limit_bytes=16 * 2**20),
        name="expert_finish",
    )(*[item[0] for item in sums])


def plane_index(y, x, c):
    return (y % N * N + x % N) * 2 + c


def leading(block, offset):
    pairs = [
        (plane_index(y, x, c), plane_index(y + offset * (1 - c), x + offset * c, c))
        for y in range(N) for x in range(N) for c in range(2)
    ]
    return lax.ppermute(block, PLANE, pairs)


def trailing(block, offset):
    pairs = [
        (plane_index(y, x, c), plane_index(y + offset * c, x + offset * (1 - c), c))
        for y in range(N) for x in range(N) for c in range(2)
    ]
    return lax.ppermute(block, PLANE, pairs)


def upright(block, offset):
    return lax.ppermute(block, "z", [(i, (i + offset) % N) for i in range(N)])


def swap(block):
    return lax.ppermute(block, "c", [(0, 1), (1, 0)])


def rolled(block, shift, dim):
    return lax.dynamic_slice_in_dim(
        jnp.concatenate([block, block], dim), shift, block.shape[dim], dim
    )


def half(block, which, dim):
    size = block.shape[dim] // 2
    return lax.dynamic_slice_in_dim(block, which * size, size, dim)


def mm(a, b):
    return jnp.dot(a, b, preferred_element_type=F32)


def three_pieces(values):
    top = lax.reduce_precision(values, 8, 7)
    middle = lax.reduce_precision(values - top, 8, 7)
    return [top, middle, values - top - middle]


def scatter_axis(chunks, send):
    arrived = [send(chunks[k], k) for k in range(1, N)]
    total = chunks[0].astype(F32)
    for block in arrived:
        total = total + block.astype(F32)
    return total


def gather_axis(block, send):
    return [block] + [send(block, -k) for k in range(1, N)]


def local(
    hidden_in, queries, cache, lengths, value_up, out_proj, norm_gain, routes, route_weight,
    w_gate, w_up, w_down,
):
    zi, yi, xi, ci = (lax.axis_index(a) for a in AXES)
    other = 1 - ci
    width = hidden_in.shape[1]
    wide = width // 2
    part = wide // 2
    requests = hidden_in.shape[0]
    chip = 2 * requests

    def chip_rows(mine, theirs):
        return jnp.concatenate(
            [jnp.where(ci == 0, mine, theirs), jnp.where(ci == 0, theirs, mine)], 0
        )

    chip_hidden = chip_rows(half(hidden_in, ci, 1), swap(half(hidden_in, other, 1)))
    gain = lax.dynamic_slice_in_dim(norm_gain, ci * wide, wide, 0)

    experts = jnp.arange(EXPERTS, dtype=jnp.int32)
    dense = jnp.sum(
        jnp.where(routes[:, :, None] == experts, route_weight[:, :, None], 0.0), 1
    )
    pieces = jnp.concatenate(three_pieces(dense) + [jnp.zeros_like(dense)], 1).astype(BF)
    chip_pieces = chip_rows(pieces, swap(pieces))

    core = ci.astype(jnp.int32).reshape(1)
    latent = attend(lengths, queries, cache)
    regrouped = lax.all_to_all(latent, PLANE, split_axis=1, concat_axis=0, tiled=True)
    _, *weights = lax.optimization_barrier((latent, w_gate[0], w_up[0], out_proj))
    sent = [half(weights[0], other, 0), half(weights[1], other, 0)]
    proj_pair, proj_own = half(weights[2], other, 1), half(weights[2], ci, 1)
    gate_other, up_other = (swap(block) for block in sent)
    regrouped, proj_pair, proj_own, sent = lax.optimization_barrier(
        (regrouped, proj_pair, proj_own, sent)
    )
    head_out = jnp.einsum("thl,hlv->thv", regrouped, value_up, preferred_element_type=F32)
    head_out = head_out.astype(BF).reshape(N, N, chip, -1)
    head_out = rolled(rolled(head_out, yi, 0), xi, 1)
    flipped = head_out.swapaxes(0, 1)
    own_order = jnp.where(ci == 0, head_out, flipped).reshape(N * N * chip, -1)
    pair_order = jnp.where(ci == 0, flipped, head_out).reshape(N * N * chip, -1)
    sent = swap(project(pair_order, proj_pair, BF))
    partial, gate_other, up_other = lax.optimization_barrier(
        (project(own_order, proj_own, F32), gate_other, up_other)
    )
    partial = partial + sent.astype(F32)
    partial = partial.astype(BF).reshape(N, N * chip, wide)
    partial, down = lax.optimization_barrier((partial, w_down[0]))
    down_sent = half(down, other, 1)
    partial = scatter_axis([partial[k] for k in range(N)], leading)
    partial, down_sent = lax.optimization_barrier((partial, down_sent))
    down_other = swap(down_sent)
    partial = partial.astype(BF).reshape(N, chip, wide)
    attended = scatter_axis([partial[k] for k in range(N)], trailing)
    residual = chip_hidden.astype(F32) + attended
    squares = jnp.sum(residual * residual, 1, keepdims=True)
    lane = jnp.arange(EXTRA, dtype=jnp.int32)
    extra = chip_pieces
    for place, piece in enumerate(three_pieces(squares)):
        extra = jnp.where(lane == 3 * EXPERTS + place, piece.astype(BF), extra)

    shard = jnp.concatenate([(residual * gain).astype(BF), extra], 1)
    shard = jnp.concatenate(gather_axis(shard, upright), 0)
    blocks = gather_axis(shard, trailing)
    near_a = jnp.concatenate(blocks[: N // 2], 0)
    near_b = jnp.concatenate(blocks[N // 2 :], 0)
    tied = near_a[:chip, :EXTRA] + near_b[:chip, :EXTRA]
    near_a, near_b, _ = lax.optimization_barrier((near_a, near_b, swap(tied)))
    before_a, after_b = leading(near_a, 1), leading(near_b, -1)
    before_b, after_a = leading(near_b, 1), leading(near_a, -1)

    place = jnp.stack([ci, plane_index(yi, xi, ci)]).astype(jnp.int32)

    def products(chunks):
        own, cross = expert_products(place, chunks, w_gate[0], w_up[0], gate_other, up_other)
        return own, swap(cross)

    sums_0 = products([near_a, near_b])
    before_a, after_b, _ = lax.optimization_barrier((before_a, after_b, sums_0[0]))
    far_a, far_b = leading(before_a, 1), leading(after_b, -1)
    sums_13 = products([after_a, after_b, before_a, before_b])
    sums_2 = products([far_a, far_b])
    own_sums, pair_sums = (
        [(sums_0[p], 0), (sums_13[p], 0), (sums_2[p], 0), (sums_13[p], near_a.shape[0] * 2)]
        for p in range(2)
    )
    hidden, flipped = expert_finish(width, near_a.shape[0] * 2, own_sums, pair_sums)
    theirs = swap(flipped)

    first = down_products([(2, 0), (2, 1), (1, 1), (3, 0)], BF, core, hidden, theirs, w_down[0], down_other)
    relay_a, relay_b = leading(first[0], 1), leading(first[1], -1)
    next_b, last_a = leading(first[2], 1), leading(first[3], -1)
    second = down_products([(1, 0), (3, 1), (0, 0), (0, 1)], F32, core, hidden, theirs, w_down[0], down_other)
    next_a = leading((second[0] + relay_a.astype(F32)).astype(BF), 1)
    last_b = leading((second[1] + relay_b.astype(F32)).astype(BF), -1)
    out_a = second[2] + last_a.astype(F32) + next_a.astype(F32)
    out_b = second[3] + next_b.astype(F32) + last_b.astype(F32)
    out = jnp.concatenate([out_a.astype(BF), out_b.astype(BF)], 1).reshape(N, N * chip, wide)
    out = scatter_axis([out[k] for k in range(N)], trailing)
    out = out.astype(BF).reshape(N, chip, wide)
    routed = scatter_axis([out[k] for k in range(N)], upright)
    layer_out = (residual + routed).astype(BF).reshape(2, requests, wide)
    mine = lax.dynamic_index_in_dim(layer_out, ci, 0, keepdims=False)
    theirs = swap(lax.dynamic_index_in_dim(layer_out, other, 0, keepdims=False))
    left = jnp.where(ci == 0, mine, theirs)
    right = jnp.where(ci == 0, theirs, mine)
    return jnp.concatenate([left, right], 1)


def solution(mesh):
    torus = Mesh(mesh.devices.reshape(N, N, N, 2), AXES)
    in_specs = (
        P(AXES, None),
        P(AXES, None, None),
        P(AXES, None),
        P(AXES),
        P(PLANE, None, None),
        P(PLANE, None),
        P(),
        P(AXES, None),
        P(AXES, None),
        P(PLANE, None, "z"),
        P(PLANE, None, "z"),
        P(PLANE, "z", None),
    )
    return jax.shard_map(
        local, mesh=torus, in_specs=in_specs, out_specs=P(AXES, None), check_vma=False
    )
```

```python
import functools

import jax
import jax.numpy as jnp
from jax import lax
from jax.experimental import pallas as pl
from jax.experimental.pallas import tpu as pltpu
from jax.sharding import Mesh, PartitionSpec as P

LAT = 512
ROPE = 64
DV = 128
LONGEST = 1024
ALIGN = 128
PIECES = 4
N = 4
EXPERTS = 32
EXTRA = 128
AXES = ("z", "y", "x", "c")
PLANE = ("y", "x", "c")
BF = jnp.bfloat16
F32 = jnp.float32


def attend_kernel(lengths, queries, cache, latent, window, gathered, arrived):
    requests, _, heads = queries.shape
    ranks = latent.shape[0]
    each = heads // ranks
    rows = window.shape[2]
    piece = window.shape[1] // PIECES
    scale = (DV + ROPE) ** (-0.5)
    begins, bases, copies = [], [], []
    begin = jnp.int32(0)
    for i in range(requests):
        base = jnp.minimum(begin // ALIGN * ALIGN, cache.shape[1] - rows)
        base = pl.multiple_of(base, ALIGN)
        copies.append([
            pltpu.make_async_copy(
                cache.at[pl.ds(j * piece, piece), pl.ds(base, rows)],
                window.at[i, pl.ds(j * piece, piece), :],
                arrived.at[i, j],
            )
            for j in range(PIECES)
        ])
        begins.append(begin)
        bases.append(base)
        begin = begin + lengths[i]
    for copy in copies[0] + copies[1]:
        copy.start()
    for i in range(requests):
        for copy in copies[i]:
            copy.wait()
        if i + 2 < requests:
            for copy in copies[i + 2]:
                copy.start()
        scores = lax.dot_general(
            queries[i], window[i], (((0,), (0,)), ((), ())), preferred_element_type=F32
        ) * scale
        place = bases[i] + lax.broadcasted_iota(jnp.int32, scores.shape, 1)
        live = (place >= begins[i]) & (place < begins[i] + lengths[i])
        scores = jnp.where(live, scores, -1e30)
        largest = jnp.max(scores, 1, keepdims=True)
        weights = jnp.where(live, jnp.exp(scores - largest), 0.0)
        totals = jnp.sum(weights, 1, keepdims=True)
        weighted = lax.dot_general(
            weights.astype(BF), window[i, :LAT, :], (((1,), (1,)), ((), ())),
            preferred_element_type=F32,
        )
        shared = (weighted / totals).reshape(ranks, each, LAT)
        gathered[:, i * each : (i + 1) * each, :] = shared
    latent[...] = gathered[...].astype(BF)


def attend(lengths, queries, cache, ranks):
    requests, heads, width = queries.shape
    rows = LONGEST + ALIGN
    shape = (ranks, requests * heads // ranks, LAT)
    vmem = pl.BlockSpec(memory_space=pltpu.VMEM)
    return pl.pallas_call(
        attend_kernel,
        out_shape=jax.ShapeDtypeStruct(shape, BF),
        in_specs=[
            pl.BlockSpec(memory_space=pltpu.SMEM), vmem, pl.BlockSpec(memory_space=pl.ANY),
        ],
        out_specs=vmem,
        scratch_shapes=[
            pltpu.VMEM((requests, width, rows), BF),
            pltpu.VMEM(shape, F32),
            pltpu.SemaphoreType.DMA((requests, PIECES)),
        ],
        compiler_params=pltpu.CompilerParams(vmem_limit_bytes=56 * 2**20),
        name="attend",
    )(lengths, queries.swapaxes(1, 2), cache.T)


def project_kernel(rows, weight, result):
    block = 512
    for k in range(result.shape[1] // block):
        here = slice(k * block, (k + 1) * block)
        product = jnp.dot(rows[...], weight[:, here], preferred_element_type=F32)
        result[:, here] = product.astype(result.dtype)


def project(rows, weight, dtype):
    count, depth = rows.shape
    wide = weight.shape[1]
    vmem = pl.BlockSpec(memory_space=pltpu.VMEM)
    return pl.pallas_call(
        project_kernel,
        out_shape=jax.ShapeDtypeStruct((count, wide), dtype),
        in_specs=[vmem, vmem],
        out_specs=vmem,
        compiler_params=pltpu.CompilerParams(vmem_limit_bytes=16 * 2**20),
        cost_estimate=pl.CostEstimate(
            flops=2 * count * depth * wide, bytes_accessed=2 * depth * wide, transcendentals=0
        ),
        name="project",
    )(rows, weight)


def down_kernel(picks, core, hidden, theirs, weight, other, *results):
    rows, part = results[0].shape

    def run(side):
        for (chunk, k), result in zip(picks, results):
            here = slice(chunk * rows, (chunk + 1) * rows)
            mine = slice((2 * side + k) * part, (2 * side + k + 1) * part)
            units = jnp.concatenate([hidden[here, :], theirs[here, :]], 1)
            weights = jnp.concatenate([weight[:, mine], other[:, k * part : (k + 1) * part]], 0)
            product = jnp.dot(units, weights, preferred_element_type=F32)
            result[...] = product.astype(result.dtype)

    for side in range(2):
        pl.when(core[0] == side)(functools.partial(run, side))


def down_products(picks, dtype, core, hidden, theirs, weight, other):
    rows, units = hidden.shape[0] // N, hidden.shape[1]
    part = other.shape[1] // 2
    vmem = pl.BlockSpec(memory_space=pltpu.VMEM)
    return pl.pallas_call(
        functools.partial(down_kernel, picks),
        out_shape=[jax.ShapeDtypeStruct((rows, part), dtype)] * len(picks),
        in_specs=[pl.BlockSpec(memory_space=pltpu.SMEM)] + [vmem] * 4,
        out_specs=[vmem] * len(picks),
        compiler_params=pltpu.CompilerParams(vmem_limit_bytes=16 * 2**20),
        cost_estimate=pl.CostEstimate(
            flops=4 * len(picks) * rows * part * units,
            bytes_accessed=2 * len(picks) * rows * part, transcendentals=0,
        ),
        name="down",
    )(core, hidden, theirs, weight, other)


def product_kernel(count, place, *refs):
    chunks, (gate, up, gate_other, up_other) = refs[:count], refs[count : count + 4]
    own_sum, cross_sum = refs[count + 4 :]
    wide, units = gate_other.shape

    def columns(begin, size):
        return jnp.concatenate([chunk[:, begin : begin + size] for chunk in chunks], 0)

    pieces = columns(wide, EXTRA).astype(F32)
    lane = lax.broadcasted_iota(jnp.int32, pieces.shape, 1)
    weighs = (lane < 3 * EXPERTS) & ((lane & (EXPERTS - 1)) == place[1])
    mix = jnp.sum(jnp.where(weighs, pieces, 0.0), 1, keepdims=True)
    squares = jnp.sum(jnp.where(lane >= 3 * EXPERTS, pieces, 0.0), 1, keepdims=True)
    own_sum[:, 2 * units :] = jnp.where(lane == 0, squares, mix)
    cross_sum[:, 2 * units :] = jnp.broadcast_to(squares, pieces.shape)
    block = 512
    for k in range(wide // block):
        here = pl.ds(k * block, block)
        mine = pl.ds(pl.multiple_of(place[0] * wide + k * block, block), block)
        tokens = columns(k * block, block)
        own = jnp.concatenate([gate[mine, :], up[mine, :]], 1)
        cross = jnp.concatenate([gate_other[here, :], up_other[here, :]], 1)
        for total, weights in ((own_sum, own), (cross_sum, cross)):
            product = jnp.dot(tokens, weights, preferred_element_type=F32)
            if k == 0:
                total[:, : 2 * units] = product
            else:
                total[:, : 2 * units] += product


def expert_products(place, chunks, w_gate, w_up, gate_other, up_other):
    depth, units = w_gate.shape
    rows = sum(chunk.shape[0] for chunk in chunks)
    vmem = pl.BlockSpec(memory_space=pltpu.VMEM)
    return pl.pallas_call(
        functools.partial(product_kernel, len(chunks)),
        out_shape=[jax.ShapeDtypeStruct((rows, 2 * units + EXTRA), F32)] * 2,
        in_specs=[pl.BlockSpec(memory_space=pltpu.SMEM)] + [vmem] * (len(chunks) + 4),
        out_specs=[vmem, vmem],
        compiler_params=pltpu.CompilerParams(vmem_limit_bytes=16 * 2**20),
        cost_estimate=pl.CostEstimate(
            flops=4 * rows * depth * units, bytes_accessed=4 * depth * units, transcendentals=0
        ),
        name="expert_products",
    )(place, *chunks, w_gate, w_up, gate_other, up_other)


def finish_kernel(width, *refs):
    own_sums, pair_sums, (hidden, flipped) = refs[:N], refs[N : 2 * N], refs[2 * N :]
    units = hidden.shape[1]
    rows = hidden.shape[0] // (N * N)
    for i in range(N):
        for j in range(N):
            own = own_sums[i][j * rows : (j + 1) * rows, :]
            pair = pair_sums[j][i * rows : (i + 1) * rows, :]
            square = own[:, 2 * units : 2 * units + 1] + pair[:, 2 * units : 2 * units + 1]
            mix = own[:, 2 * units + 1 : 2 * units + 2]
            factor = lax.rsqrt(square / width + 1e-06)
            both = (own[:, : 2 * units] + pair[:, : 2 * units]) * factor
            gate, up = both[:, :units], both[:, units:]
            acted = (gate / (1.0 + jnp.exp(-gate)) * up * mix).astype(BF)
            hidden[(i * N + j) * rows : (i * N + j + 1) * rows, :] = acted
            flipped[(j * N + i) * rows : (j * N + i + 1) * rows, :] = acted


def expert_finish(width, rows, own_sums, pair_sums):
    columns = own_sums[0][0].shape[1]
    units = (columns - EXTRA) // 2

    def sums_spec(item):
        index = item[1] // rows
        return pl.BlockSpec((rows, columns), lambda k: (index, 0))

    whole = pl.BlockSpec((N * rows, units), lambda k: (0, 0))
    sums = list(own_sums) + list(pair_sums)
    return pl.pallas_call(
        functools.partial(finish_kernel, width),
        out_shape=[jax.ShapeDtypeStruct((N * rows, units), BF)] * 2,
        grid=(1,),
        in_specs=[sums_spec(item) for item in sums],
        out_specs=[whole, whole],
        compiler_params=pltpu.CompilerParams(vmem_limit_bytes=16 * 2**20),
        name="expert_finish",
    )(*[item[0] for item in sums])


def plane_index(y, x, c):
    return (y % N * N + x % N) * 2 + c


def leading(block, offset):
    pairs = [
        (plane_index(y, x, c), plane_index(y + offset * (1 - c), x + offset * c, c))
        for y in range(N) for x in range(N) for c in range(2)
    ]
    return lax.ppermute(block, PLANE, pairs)


def trailing(block, offset):
    pairs = [
        (plane_index(y, x, c), plane_index(y + offset * c, x + offset * (1 - c), c))
        for y in range(N) for x in range(N) for c in range(2)
    ]
    return lax.ppermute(block, PLANE, pairs)


def upright(block, offset):
    return lax.ppermute(block, "z", [(i, (i + offset) % N) for i in range(N)])


def swap(block):
    return lax.ppermute(block, "c", [(0, 1), (1, 0)])


def rolled(block, shift, dim):
    return lax.dynamic_slice_in_dim(
        jnp.concatenate([block, block], dim), shift, block.shape[dim], dim
    )


def half(block, which, dim):
    size = block.shape[dim] // 2
    return lax.dynamic_slice_in_dim(block, which * size, size, dim)


def mm(a, b):
    return jnp.dot(a, b, preferred_element_type=F32)


def three_pieces(values):
    top = lax.reduce_precision(values, 8, 7)
    middle = lax.reduce_precision(values - top, 8, 7)
    return [top, middle, values - top - middle]


def scatter_axis(chunks, send):
    arrived = [send(chunks[k], k) for k in range(1, N)]
    total = chunks[0].astype(F32)
    for block in arrived:
        total = total + block.astype(F32)
    return total


def gather_axis(block, send):
    return [block] + [send(block, -k) for k in range(1, N)]


def local(
    hidden_in, queries, cache, lengths, value_up, out_proj, norm_gain, routes, route_weight,
    w_gate, w_up, w_down,
):
    zi, yi, xi, ci = (lax.axis_index(a) for a in AXES)
    other = 1 - ci
    width = hidden_in.shape[1]
    wide = width // 2
    part = wide // 2
    requests = hidden_in.shape[0]
    chip = 2 * requests

    def chip_rows(mine, theirs):
        return jnp.concatenate(
            [jnp.where(ci == 0, mine, theirs), jnp.where(ci == 0, theirs, mine)], 0
        )

    chip_hidden = chip_rows(half(hidden_in, ci, 1), swap(half(hidden_in, other, 1)))
    gain = lax.dynamic_slice_in_dim(norm_gain, ci * wide, wide, 0)

    experts = jnp.arange(EXPERTS, dtype=jnp.int32)
    dense = jnp.sum(
        jnp.where(routes[:, :, None] == experts, route_weight[:, :, None], 0.0), 1
    )
    pieces = jnp.concatenate(three_pieces(dense) + [jnp.zeros_like(dense)], 1).astype(BF)
    chip_pieces = chip_rows(pieces, swap(pieces))

    core = ci.astype(jnp.int32).reshape(1)
    ranks = N * N * 2
    latent = attend(lengths, queries, cache, ranks)
    regrouped = lax.all_to_all(latent, PLANE, split_axis=0, concat_axis=0, tiled=True)
    regrouped = regrouped.reshape(ranks * requests, -1, LAT)
    _, *weights = lax.optimization_barrier((latent, w_gate[0], w_up[0], out_proj))
    sent = [half(weights[0], other, 0), half(weights[1], other, 0)]
    proj_pair, proj_own = half(weights[2], other, 1), half(weights[2], ci, 1)
    gate_other, up_other = (swap(block) for block in sent)
    regrouped, proj_pair, proj_own, sent = lax.optimization_barrier(
        (regrouped, proj_pair, proj_own, sent)
    )
    head_out = jnp.einsum("thl,hlv->thv", regrouped, value_up, preferred_element_type=F32)
    head_out = head_out.astype(BF).reshape(N, N, chip, -1)
    head_out = rolled(rolled(head_out, yi, 0), xi, 1)
    flipped = head_out.swapaxes(0, 1)
    own_order = jnp.where(ci == 0, head_out, flipped).reshape(N * N * chip, -1)
    pair_order = jnp.where(ci == 0, flipped, head_out).reshape(N * N * chip, -1)
    sent = swap(project(pair_order, proj_pair, BF))
    partial, gate_other, up_other = lax.optimization_barrier(
        (project(own_order, proj_own, F32), gate_other, up_other)
    )
    partial = partial + sent.astype(F32)
    partial = partial.astype(BF).reshape(N, N * chip, wide)
    partial, down = lax.optimization_barrier((partial, w_down[0]))
    down_sent = half(down, other, 1)
    partial = scatter_axis([partial[k] for k in range(N)], leading)
    partial, down_sent = lax.optimization_barrier((partial, down_sent))
    down_other = swap(down_sent)
    partial = partial.astype(BF).reshape(N, chip, wide)
    attended = scatter_axis([partial[k] for k in range(N)], trailing)
    residual = chip_hidden.astype(F32) + attended
    squares = jnp.sum(residual * residual, 1, keepdims=True)
    lane = jnp.arange(EXTRA, dtype=jnp.int32)
    extra = chip_pieces
    for place, piece in enumerate(three_pieces(squares)):
        extra = jnp.where(lane == 3 * EXPERTS + place, piece.astype(BF), extra)

    shard = jnp.concatenate([(residual * gain).astype(BF), extra], 1)
    shard = jnp.concatenate(gather_axis(shard, upright), 0)
    blocks = gather_axis(shard, trailing)
    near_a = jnp.concatenate(blocks[: N // 2], 0)
    near_b = jnp.concatenate(blocks[N // 2 :], 0)
    tied = near_a[:chip, :EXTRA] + near_b[:chip, :EXTRA]
    near_a, near_b, _ = lax.optimization_barrier((near_a, near_b, swap(tied)))
    before_a, after_b = leading(near_a, 1), leading(near_b, -1)
    before_b, after_a = leading(near_b, 1), leading(near_a, -1)

    place = jnp.stack([ci, plane_index(yi, xi, ci)]).astype(jnp.int32)

    def products(chunks):
        own, cross = expert_products(place, chunks, w_gate[0], w_up[0], gate_other, up_other)
        return own, swap(cross)

    sums_0 = products([near_a, near_b])
    before_a, after_b, _ = lax.optimization_barrier((before_a, after_b, sums_0[0]))
    far_a, far_b = leading(before_a, 1), leading(after_b, -1)
    sums_13 = products([after_a, after_b, before_a, before_b])
    sums_2 = products([far_a, far_b])
    own_sums, pair_sums = (
        [(sums_0[p], 0), (sums_13[p], 0), (sums_2[p], 0), (sums_13[p], near_a.shape[0] * 2)]
        for p in range(2)
    )
    hidden, flipped = expert_finish(width, near_a.shape[0] * 2, own_sums, pair_sums)
    theirs = swap(flipped)

    def products_down(picks, dtype):
        return down_products(picks, dtype, core, hidden, theirs, w_down[0], down_other)

    far = products_down([(2, 0), (2, 1)], BF)
    relay_a, relay_b = leading(far[0], 1), leading(far[1], -1)
    near = products_down([(1, 1), (3, 0)], BF)
    next_b, last_a = leading(near[0], 1), leading(near[1], -1)
    second = products_down([(1, 0), (3, 1), (0, 0), (0, 1)], F32)
    next_a = leading((second[0] + relay_a.astype(F32)).astype(BF), 1)
    last_b = leading((second[1] + relay_b.astype(F32)).astype(BF), -1)
    out_a = second[2] + last_a.astype(F32) + next_a.astype(F32)
    out_b = second[3] + next_b.astype(F32) + last_b.astype(F32)
    out = jnp.concatenate([out_a.astype(BF), out_b.astype(BF)], 1).reshape(N, N * chip, wide)
    out, _ = lax.optimization_barrier((out, swap(out[0, :chip, :EXTRA])))
    out = scatter_axis([out[k] for k in range(N)], trailing)
    out = out.astype(BF).reshape(N, chip, wide)
    routed = scatter_axis([out[k] for k in range(N)], upright)
    layer_out = (residual + routed).astype(BF).reshape(2, requests, wide)
    mine = lax.dynamic_index_in_dim(layer_out, ci, 0, keepdims=False)
    theirs = swap(lax.dynamic_index_in_dim(layer_out, other, 0, keepdims=False))
    left = jnp.where(ci == 0, mine, theirs)
    right = jnp.where(ci == 0, theirs, mine)
    return jnp.concatenate([left, right], 1)


def solution(mesh):
    torus = Mesh(mesh.devices.reshape(N, N, N, 2), AXES)
    in_specs = (
        P(AXES, None),
        P(AXES, None, None),
        P(AXES, None),
        P(AXES),
        P(PLANE, None, None),
        P(PLANE, None),
        P(),
        P(AXES, None),
        P(AXES, None),
        P(PLANE, None, "z"),
        P(PLANE, None, "z"),
        P(PLANE, "z", None),
    )
    return jax.shard_map(
        local, mesh=torus, in_specs=in_specs, out_specs=P(AXES, None), check_vma=False
    )
```

```python
import functools

import jax
import jax.numpy as jnp
from jax import lax
from jax.experimental import pallas as pl
from jax.experimental.pallas import tpu as pltpu
from jax.sharding import Mesh, PartitionSpec as P

LAT = 512
ROPE = 64
DV = 128
LONGEST = 1024
ALIGN = 128
PIECES = 4
N = 4
EXPERTS = 32
EXTRA = 128
AXES = ("z", "y", "x", "c")
PLANE = ("y", "x", "c")
BF = jnp.bfloat16
F32 = jnp.float32


def attend_kernel(lengths, queries, cache, latent, window, gathered, arrived):
    requests, _, heads = queries.shape
    ranks = latent.shape[0]
    each = heads // ranks
    rows = window.shape[2]
    piece = window.shape[1] // PIECES
    scale = (DV + ROPE) ** (-0.5)
    begins, bases, copies = [], [], []
    begin = jnp.int32(0)
    for i in range(requests):
        base = jnp.minimum(begin // ALIGN * ALIGN, cache.shape[1] - rows)
        base = pl.multiple_of(base, ALIGN)
        copies.append([
            pltpu.make_async_copy(
                cache.at[pl.ds(j * piece, piece), pl.ds(base, rows)],
                window.at[i, pl.ds(j * piece, piece), :],
                arrived.at[i, j],
            )
            for j in range(PIECES)
        ])
        begins.append(begin)
        bases.append(base)
        begin = begin + lengths[i]
    for copy in copies[0] + copies[1]:
        copy.start()
    for i in range(requests):
        for copy in copies[i]:
            copy.wait()
        if i + 2 < requests:
            for copy in copies[i + 2]:
                copy.start()
        scores = lax.dot_general(
            queries[i], window[i], (((0,), (0,)), ((), ())), preferred_element_type=F32
        ) * scale
        place = bases[i] + lax.broadcasted_iota(jnp.int32, scores.shape, 1)
        live = (place >= begins[i]) & (place < begins[i] + lengths[i])
        scores = jnp.where(live, scores, -1e30)
        largest = jnp.max(scores, 1, keepdims=True)
        weights = jnp.where(live, jnp.exp(scores - largest), 0.0)
        totals = jnp.sum(weights, 1, keepdims=True)
        weighted = lax.dot_general(
            weights.astype(BF), window[i, :LAT, :], (((1,), (1,)), ((), ())),
            preferred_element_type=F32,
        )
        shared = (weighted / totals).reshape(ranks, each, LAT)
        gathered[:, i * each : (i + 1) * each, :] = shared
    latent[...] = gathered[...].astype(BF)


def attend(lengths, queries, cache, ranks):
    requests, heads, width = queries.shape
    rows = LONGEST + ALIGN
    shape = (ranks, requests * heads // ranks, LAT)
    vmem = pl.BlockSpec(memory_space=pltpu.VMEM)
    return pl.pallas_call(
        attend_kernel,
        out_shape=jax.ShapeDtypeStruct(shape, BF),
        in_specs=[
            pl.BlockSpec(memory_space=pltpu.SMEM), vmem, pl.BlockSpec(memory_space=pl.ANY),
        ],
        out_specs=vmem,
        scratch_shapes=[
            pltpu.VMEM((requests, width, rows), BF),
            pltpu.VMEM(shape, F32),
            pltpu.SemaphoreType.DMA((requests, PIECES)),
        ],
        compiler_params=pltpu.CompilerParams(vmem_limit_bytes=56 * 2**20),
        name="attend",
    )(lengths, queries.swapaxes(1, 2), cache.T)


def project_kernel(rows, weight, result):
    block = 512
    for k in range(result.shape[1] // block):
        here = slice(k * block, (k + 1) * block)
        product = jnp.dot(rows[...], weight[:, here], preferred_element_type=F32)
        result[:, here] = product.astype(result.dtype)


def project(rows, weight, dtype):
    count, depth = rows.shape
    wide = weight.shape[1]
    vmem = pl.BlockSpec(memory_space=pltpu.VMEM)
    return pl.pallas_call(
        project_kernel,
        out_shape=jax.ShapeDtypeStruct((count, wide), dtype),
        in_specs=[vmem, vmem],
        out_specs=vmem,
        compiler_params=pltpu.CompilerParams(vmem_limit_bytes=16 * 2**20),
        cost_estimate=pl.CostEstimate(
            flops=2 * count * depth * wide, bytes_accessed=2 * depth * wide, transcendentals=0
        ),
        name="project",
    )(rows, weight)


def down_kernel(picks, core, hidden, theirs, weight, other, *results):
    rows, part = results[0].shape

    def run(side):
        for (chunk, k), result in zip(picks, results):
            here = slice(chunk * rows, (chunk + 1) * rows)
            mine = slice((2 * side + k) * part, (2 * side + k + 1) * part)
            units = jnp.concatenate([hidden[here, :], theirs[here, :]], 1)
            weights = jnp.concatenate([weight[:, mine], other[:, k * part : (k + 1) * part]], 0)
            product = jnp.dot(units, weights, preferred_element_type=F32)
            result[...] = product.astype(result.dtype)

    for side in range(2):
        pl.when(core[0] == side)(functools.partial(run, side))


def down_products(picks, dtype, core, hidden, theirs, weight, other):
    rows, units = hidden.shape[0] // N, hidden.shape[1]
    part = other.shape[1] // 2
    vmem = pl.BlockSpec(memory_space=pltpu.VMEM)
    return pl.pallas_call(
        functools.partial(down_kernel, picks),
        out_shape=[jax.ShapeDtypeStruct((rows, part), dtype)] * len(picks),
        in_specs=[pl.BlockSpec(memory_space=pltpu.SMEM)] + [vmem] * 4,
        out_specs=[vmem] * len(picks),
        compiler_params=pltpu.CompilerParams(vmem_limit_bytes=16 * 2**20),
        cost_estimate=pl.CostEstimate(
            flops=4 * len(picks) * rows * part * units,
            bytes_accessed=2 * len(picks) * rows * part, transcendentals=0,
        ),
        name="down",
    )(core, hidden, theirs, weight, other)


def product_kernel(count, place, *refs):
    chunks, (gate, up, gate_other, up_other) = refs[:count], refs[count : count + 4]
    own_sum, cross_sum = refs[count + 4 :]
    wide, units = gate_other.shape

    def columns(begin, size):
        return jnp.concatenate([chunk[:, begin : begin + size] for chunk in chunks], 0)

    pieces = columns(wide, EXTRA).astype(F32)
    lane = lax.broadcasted_iota(jnp.int32, pieces.shape, 1)
    weighs = (lane < 3 * EXPERTS) & ((lane & (EXPERTS - 1)) == place[1])
    mix = jnp.sum(jnp.where(weighs, pieces, 0.0), 1, keepdims=True)
    squares = jnp.sum(jnp.where(lane >= 3 * EXPERTS, pieces, 0.0), 1, keepdims=True)
    own_sum[:, 2 * units :] = jnp.where(lane == 0, squares, mix)
    cross_sum[:, 2 * units :] = jnp.broadcast_to(squares, pieces.shape)
    block = 512
    for k in range(wide // block):
        here = pl.ds(k * block, block)
        mine = pl.ds(pl.multiple_of(place[0] * wide + k * block, block), block)
        tokens = columns(k * block, block)
        own = jnp.concatenate([gate[mine, :], up[mine, :]], 1)
        cross = jnp.concatenate([gate_other[here, :], up_other[here, :]], 1)
        for total, weights in ((own_sum, own), (cross_sum, cross)):
            product = jnp.dot(tokens, weights, preferred_element_type=F32)
            if k == 0:
                total[:, : 2 * units] = product
            else:
                total[:, : 2 * units] += product


def expert_products(place, chunks, w_gate, w_up, gate_other, up_other):
    depth, units = w_gate.shape
    rows = sum(chunk.shape[0] for chunk in chunks)
    vmem = pl.BlockSpec(memory_space=pltpu.VMEM)
    return pl.pallas_call(
        functools.partial(product_kernel, len(chunks)),
        out_shape=[jax.ShapeDtypeStruct((rows, 2 * units + EXTRA), F32)] * 2,
        in_specs=[pl.BlockSpec(memory_space=pltpu.SMEM)] + [vmem] * (len(chunks) + 4),
        out_specs=[vmem, vmem],
        compiler_params=pltpu.CompilerParams(vmem_limit_bytes=16 * 2**20),
        cost_estimate=pl.CostEstimate(
            flops=4 * rows * depth * units, bytes_accessed=4 * depth * units, transcendentals=0
        ),
        name="expert_products",
    )(place, *chunks, w_gate, w_up, gate_other, up_other)


def finish_kernel(width, *refs):
    own_sums, pair_sums, (hidden, flipped) = refs[:N], refs[N : 2 * N], refs[2 * N :]
    units = hidden.shape[1]
    rows = hidden.shape[0] // (N * N)
    for i in range(N):
        for j in range(N):
            own = own_sums[i][j * rows : (j + 1) * rows, :]
            pair = pair_sums[j][i * rows : (i + 1) * rows, :]
            square = own[:, 2 * units : 2 * units + 1] + pair[:, 2 * units : 2 * units + 1]
            mix = own[:, 2 * units + 1 : 2 * units + 2]
            factor = lax.rsqrt(square / width + 1e-06)
            both = (own[:, : 2 * units] + pair[:, : 2 * units]) * factor
            gate, up = both[:, :units], both[:, units:]
            acted = (gate / (1.0 + jnp.exp(-gate)) * up * mix).astype(BF)
            hidden[(i * N + j) * rows : (i * N + j + 1) * rows, :] = acted
            flipped[(j * N + i) * rows : (j * N + i + 1) * rows, :] = acted


def expert_finish(width, rows, own_sums, pair_sums):
    columns = own_sums[0][0].shape[1]
    units = (columns - EXTRA) // 2

    def sums_spec(item):
        index = item[1] // rows
        return pl.BlockSpec((rows, columns), lambda k: (index, 0))

    whole = pl.BlockSpec((N * rows, units), lambda k: (0, 0))
    sums = list(own_sums) + list(pair_sums)
    return pl.pallas_call(
        functools.partial(finish_kernel, width),
        out_shape=[jax.ShapeDtypeStruct((N * rows, units), BF)] * 2,
        grid=(1,),
        in_specs=[sums_spec(item) for item in sums],
        out_specs=[whole, whole],
        compiler_params=pltpu.CompilerParams(vmem_limit_bytes=16 * 2**20),
        name="expert_finish",
    )(*[item[0] for item in sums])


def plane_index(y, x, c):
    return (y % N * N + x % N) * 2 + c


def leading(block, offset):
    pairs = [
        (plane_index(y, x, c), plane_index(y + offset * (1 - c), x + offset * c, c))
        for y in range(N) for x in range(N) for c in range(2)
    ]
    return lax.ppermute(block, PLANE, pairs)


def trailing(block, offset):
    pairs = [
        (plane_index(y, x, c), plane_index(y + offset * c, x + offset * (1 - c), c))
        for y in range(N) for x in range(N) for c in range(2)
    ]
    return lax.ppermute(block, PLANE, pairs)


def upright(block, offset):
    return lax.ppermute(block, "z", [(i, (i + offset) % N) for i in range(N)])


def swap(block):
    return lax.ppermute(block, "c", [(0, 1), (1, 0)])


def rolled(block, shift, dim):
    return lax.dynamic_slice_in_dim(
        jnp.concatenate([block, block], dim), shift, block.shape[dim], dim
    )


def half(block, which, dim):
    size = block.shape[dim] // 2
    return lax.dynamic_slice_in_dim(block, which * size, size, dim)


def mm(a, b):
    return jnp.dot(a, b, preferred_element_type=F32)


def three_pieces(values):
    top = lax.reduce_precision(values, 8, 7)
    middle = lax.reduce_precision(values - top, 8, 7)
    return [top, middle, values - top - middle]


def scatter_axis(chunks, send):
    arrived = [send(chunks[k], k) for k in range(1, N)]
    total = chunks[0].astype(F32)
    for block in arrived:
        total = total + block.astype(F32)
    return total


def gather_axis(block, send):
    return [block] + [send(block, -k) for k in range(1, N)]


def local(
    hidden_in, queries, cache, lengths, value_up, out_proj, norm_gain, routes, route_weight,
    w_gate, w_up, w_down,
):
    zi, yi, xi, ci = (lax.axis_index(a) for a in AXES)
    other = 1 - ci
    width = hidden_in.shape[1]
    wide = width // 2
    part = wide // 2
    requests = hidden_in.shape[0]
    chip = 2 * requests

    def chip_rows(mine, theirs):
        return jnp.concatenate(
            [jnp.where(ci == 0, mine, theirs), jnp.where(ci == 0, theirs, mine)], 0
        )

    gain = lax.dynamic_slice_in_dim(norm_gain, ci * wide, wide, 0)

    experts = jnp.arange(EXPERTS, dtype=jnp.int32)
    dense = jnp.sum(
        jnp.where(routes[:, :, None] == experts, route_weight[:, :, None], 0.0), 1
    )
    pieces = jnp.concatenate(three_pieces(dense) + [jnp.zeros_like(dense)], 1).astype(BF)

    core = ci.astype(jnp.int32).reshape(1)
    ranks = N * N * 2
    latent = attend(lengths, queries, cache, ranks)
    regrouped = lax.all_to_all(latent, PLANE, split_axis=0, concat_axis=0, tiled=True)
    regrouped = regrouped.reshape(ranks * requests, -1, LAT)
    _, *weights = lax.optimization_barrier((latent, w_gate[0], w_up[0], out_proj))
    sent = [half(weights[0], other, 0), half(weights[1], other, 0)]
    proj_pair, proj_own = half(weights[2], other, 1), half(weights[2], ci, 1)
    gate_other, up_other = (swap(block) for block in sent)
    regrouped, proj_pair, proj_own, sent = lax.optimization_barrier(
        (regrouped, proj_pair, proj_own, sent)
    )
    head_out = jnp.einsum("thl,hlv->thv", regrouped, value_up, preferred_element_type=F32)
    head_out = head_out.astype(BF).reshape(N, N, chip, -1)
    head_out = rolled(rolled(head_out, yi, 0), xi, 1)
    flipped = head_out.swapaxes(0, 1)
    own_order = jnp.where(ci == 0, head_out, flipped).reshape(N * N * chip, -1)
    pair_order = jnp.where(ci == 0, flipped, head_out).reshape(N * N * chip, -1)
    sent = swap(project(pair_order, proj_pair, BF))
    partial, gate_other, up_other = lax.optimization_barrier(
        (project(own_order, proj_own, F32), gate_other, up_other)
    )
    partial = partial + sent.astype(F32)
    partial = partial.astype(BF).reshape(N, N * chip, wide)
    partial, down, hidden_in, pieces = lax.optimization_barrier(
        (partial, w_down[0], hidden_in, pieces)
    )
    chip_hidden = chip_rows(half(hidden_in, ci, 1), swap(half(hidden_in, other, 1)))
    chip_pieces = chip_rows(pieces, swap(pieces))
    down_sent = half(down, other, 1)
    partial = scatter_axis([partial[k] for k in range(N)], leading)
    partial, down_sent = lax.optimization_barrier((partial, down_sent))
    down_other = swap(down_sent)
    partial = partial.astype(BF).reshape(N, chip, wide)
    attended = scatter_axis([partial[k] for k in range(N)], trailing)
    residual = chip_hidden.astype(F32) + attended
    squares = jnp.sum(residual * residual, 1, keepdims=True)
    lane = jnp.arange(EXTRA, dtype=jnp.int32)
    extra = chip_pieces
    for place, piece in enumerate(three_pieces(squares)):
        extra = jnp.where(lane == 3 * EXPERTS + place, piece.astype(BF), extra)

    shard = jnp.concatenate([(residual * gain).astype(BF), extra], 1)
    shard = jnp.concatenate(gather_axis(shard, upright), 0)
    blocks = gather_axis(shard, trailing)
    near_a = jnp.concatenate(blocks[: N // 2], 0)
    near_b = jnp.concatenate(blocks[N // 2 :], 0)
    tied = near_a[:chip, :EXTRA] + near_b[:chip, :EXTRA]
    near_a, near_b, _ = lax.optimization_barrier((near_a, near_b, swap(tied)))
    before_a, after_b = leading(near_a, 1), leading(near_b, -1)
    before_b, after_a = leading(near_b, 1), leading(near_a, -1)

    place = jnp.stack([ci, plane_index(yi, xi, ci)]).astype(jnp.int32)

    def products(chunks):
        own, cross = expert_products(place, chunks, w_gate[0], w_up[0], gate_other, up_other)
        return own, swap(cross)

    sums_0 = products([near_a, near_b])
    before_a, after_b, _ = lax.optimization_barrier((before_a, after_b, sums_0[0]))
    far_a, far_b = leading(before_a, 1), leading(after_b, -1)
    sums_13 = products([after_a, after_b, before_a, before_b])
    sums_2 = products([far_a, far_b])
    own_sums, pair_sums = (
        [(sums_0[p], 0), (sums_13[p], 0), (sums_2[p], 0), (sums_13[p], near_a.shape[0] * 2)]
        for p in range(2)
    )
    hidden, flipped = expert_finish(width, near_a.shape[0] * 2, own_sums, pair_sums)
    theirs = swap(flipped)

    def products_down(picks, dtype):
        return down_products(picks, dtype, core, hidden, theirs, w_down[0], down_other)

    far = products_down([(2, 0), (2, 1)], BF)
    relay_a, relay_b = leading(far[0], 1), leading(far[1], -1)
    near = products_down([(1, 1), (3, 0)], BF)
    next_b, last_a = leading(near[0], 1), leading(near[1], -1)
    second = products_down([(1, 0), (3, 1), (0, 0), (0, 1)], F32)
    next_a = leading((second[0] + relay_a.astype(F32)).astype(BF), 1)
    last_b = leading((second[1] + relay_b.astype(F32)).astype(BF), -1)
    out_a = second[2] + last_a.astype(F32) + next_a.astype(F32)
    out_b = second[3] + next_b.astype(F32) + last_b.astype(F32)
    out = jnp.concatenate([out_a.astype(BF), out_b.astype(BF)], 1).reshape(N, N * chip, wide)
    out, _ = lax.optimization_barrier((out, swap(out[0, :chip, :EXTRA])))
    out = scatter_axis([out[k] for k in range(N)], trailing)
    out = out.astype(BF).reshape(N, chip, wide)
    routed = scatter_axis([out[k] for k in range(N)], upright)
    layer_out = (residual + routed).astype(BF).reshape(2, requests, wide)
    mine = lax.dynamic_index_in_dim(layer_out, ci, 0, keepdims=False)
    theirs = swap(lax.dynamic_index_in_dim(layer_out, other, 0, keepdims=False))
    left = jnp.where(ci == 0, mine, theirs)
    right = jnp.where(ci == 0, theirs, mine)
    return jnp.concatenate([left, right], 1)


def solution(mesh):
    torus = Mesh(mesh.devices.reshape(N, N, N, 2), AXES)
    in_specs = (
        P(AXES, None),
        P(AXES, None, None),
        P(AXES, None),
        P(AXES),
        P(PLANE, None, None),
        P(PLANE, None),
        P(),
        P(AXES, None),
        P(AXES, None),
        P(PLANE, None, "z"),
        P(PLANE, None, "z"),
        P(PLANE, "z", None),
    )
    return jax.shard_map(
        local, mesh=torus, in_specs=in_specs, out_specs=P(AXES, None), check_vma=False
    )
```

```python
import functools

import jax
import jax.numpy as jnp
from jax import lax
from jax.experimental import pallas as pl
from jax.experimental.pallas import tpu as pltpu
from jax.sharding import Mesh, PartitionSpec as P

LAT = 512
ROPE = 64
DV = 128
LONGEST = 1024
ALIGN = 128
PIECES = 4
N = 4
EXPERTS = 32
EXTRA = 128
AXES = ("z", "y", "x", "c")
PLANE = ("y", "x", "c")
BF = jnp.bfloat16
F32 = jnp.float32


def attend_kernel(lengths, queries, cache, latent, window, gathered, arrived):
    requests, _, heads = queries.shape
    ranks = latent.shape[0]
    each = heads // ranks
    rows = window.shape[2]
    piece = window.shape[1] // PIECES
    scale = (DV + ROPE) ** (-0.5)
    begins, bases, copies = [], [], []
    begin = jnp.int32(0)
    for i in range(requests):
        base = jnp.minimum(begin // ALIGN * ALIGN, cache.shape[1] - rows)
        base = pl.multiple_of(base, ALIGN)
        copies.append([
            pltpu.make_async_copy(
                cache.at[pl.ds(j * piece, piece), pl.ds(base, rows)],
                window.at[i, pl.ds(j * piece, piece), :],
                arrived.at[i, j],
            )
            for j in range(PIECES)
        ])
        begins.append(begin)
        bases.append(base)
        begin = begin + lengths[i]
    for copy in copies[0] + copies[1]:
        copy.start()
    for i in range(requests):
        for copy in copies[i]:
            copy.wait()
        if i + 2 < requests:
            for copy in copies[i + 2]:
                copy.start()
        scores = lax.dot_general(
            queries[i], window[i], (((0,), (0,)), ((), ())), preferred_element_type=F32
        ) * scale
        place = bases[i] + lax.broadcasted_iota(jnp.int32, scores.shape, 1)
        live = (place >= begins[i]) & (place < begins[i] + lengths[i])
        scores = jnp.where(live, scores, -1e30)
        largest = jnp.max(scores, 1, keepdims=True)
        weights = jnp.where(live, jnp.exp(scores - largest), 0.0)
        totals = jnp.sum(weights, 1, keepdims=True)
        weighted = lax.dot_general(
            weights.astype(BF), window[i, :LAT, :], (((1,), (1,)), ((), ())),
            preferred_element_type=F32,
        )
        shared = (weighted / totals).reshape(ranks, each, LAT)
        gathered[:, i * each : (i + 1) * each, :] = shared
    latent[...] = gathered[...].astype(BF)


def attend(lengths, queries, cache, ranks):
    requests, heads, width = queries.shape
    rows = LONGEST + ALIGN
    shape = (ranks, requests * heads // ranks, LAT)
    vmem = pl.BlockSpec(memory_space=pltpu.VMEM)
    return pl.pallas_call(
        attend_kernel,
        out_shape=jax.ShapeDtypeStruct(shape, BF),
        in_specs=[
            pl.BlockSpec(memory_space=pltpu.SMEM), vmem, pl.BlockSpec(memory_space=pl.ANY),
        ],
        out_specs=vmem,
        scratch_shapes=[
            pltpu.VMEM((requests, width, rows), BF),
            pltpu.VMEM(shape, F32),
            pltpu.SemaphoreType.DMA((requests, PIECES)),
        ],
        compiler_params=pltpu.CompilerParams(vmem_limit_bytes=56 * 2**20),
        name="attend",
    )(lengths, queries.swapaxes(1, 2), cache.T)


def project_kernel(rows, weight, result):
    block = 512
    for k in range(result.shape[1] // block):
        here = slice(k * block, (k + 1) * block)
        product = jnp.dot(rows[...], weight[:, here], preferred_element_type=F32)
        result[:, here] = product.astype(result.dtype)


def project(rows, weight, dtype):
    count, depth = rows.shape
    wide = weight.shape[1]
    vmem = pl.BlockSpec(memory_space=pltpu.VMEM)
    return pl.pallas_call(
        project_kernel,
        out_shape=jax.ShapeDtypeStruct((count, wide), dtype),
        in_specs=[vmem, vmem],
        out_specs=vmem,
        compiler_params=pltpu.CompilerParams(vmem_limit_bytes=16 * 2**20),
        cost_estimate=pl.CostEstimate(
            flops=2 * count * depth * wide, bytes_accessed=2 * depth * wide, transcendentals=0
        ),
        name="project",
    )(rows, weight)


def down_kernel(picks, core, hidden, theirs, weight, other, *results):
    rows, part = results[0].shape

    def run(side):
        for (chunk, k), result in zip(picks, results):
            here = slice(chunk * rows, (chunk + 1) * rows)
            mine = slice((2 * side + k) * part, (2 * side + k + 1) * part)
            units = jnp.concatenate([hidden[here, :], theirs[here, :]], 1)
            weights = jnp.concatenate([weight[:, mine], other[:, k * part : (k + 1) * part]], 0)
            product = jnp.dot(units, weights, preferred_element_type=F32)
            result[...] = product.astype(result.dtype)

    for side in range(2):
        pl.when(core[0] == side)(functools.partial(run, side))


def down_products(picks, dtype, core, hidden, theirs, weight, other):
    rows, units = hidden.shape[0] // N, hidden.shape[1]
    part = other.shape[1] // 2
    vmem = pl.BlockSpec(memory_space=pltpu.VMEM)
    return pl.pallas_call(
        functools.partial(down_kernel, picks),
        out_shape=[jax.ShapeDtypeStruct((rows, part), dtype)] * len(picks),
        in_specs=[pl.BlockSpec(memory_space=pltpu.SMEM)] + [vmem] * 4,
        out_specs=[vmem] * len(picks),
        compiler_params=pltpu.CompilerParams(vmem_limit_bytes=16 * 2**20),
        cost_estimate=pl.CostEstimate(
            flops=4 * len(picks) * rows * part * units,
            bytes_accessed=2 * len(picks) * rows * part, transcendentals=0,
        ),
        name="down",
    )(core, hidden, theirs, weight, other)


def product_kernel(count, place, *refs):
    chunks, (gate, up, gate_other, up_other) = refs[:count], refs[count : count + 4]
    own_sum, cross_sum = refs[count + 4 :]
    wide, units = gate_other.shape

    def columns(begin, size):
        return jnp.concatenate([chunk[:, begin : begin + size] for chunk in chunks], 0)

    pieces = columns(wide, EXTRA).astype(F32)
    lane = lax.broadcasted_iota(jnp.int32, pieces.shape, 1)
    weighs = (lane < 3 * EXPERTS) & ((lane & (EXPERTS - 1)) == place[1])
    mix = jnp.sum(jnp.where(weighs, pieces, 0.0), 1, keepdims=True)
    squares = jnp.sum(jnp.where(lane >= 3 * EXPERTS, pieces, 0.0), 1, keepdims=True)
    own_sum[:, 2 * units :] = jnp.where(lane == 0, squares, mix)
    cross_sum[:, 2 * units :] = jnp.broadcast_to(squares, pieces.shape)
    block = 1792
    for k in range(wide // block):
        here = pl.ds(k * block, block)
        mine = pl.ds(pl.multiple_of(place[0] * wide + k * block, block), block)
        tokens = columns(k * block, block)
        own = jnp.concatenate([gate[mine, :], up[mine, :]], 1)
        cross = jnp.concatenate([gate_other[here, :], up_other[here, :]], 1)
        for total, weights in ((own_sum, own), (cross_sum, cross)):
            product = jnp.dot(tokens, weights, preferred_element_type=F32)
            if k == 0:
                total[:, : 2 * units] = product
            else:
                total[:, : 2 * units] += product


def expert_products(place, chunks, w_gate, w_up, gate_other, up_other):
    depth, units = w_gate.shape
    rows = sum(chunk.shape[0] for chunk in chunks)
    vmem = pl.BlockSpec(memory_space=pltpu.VMEM)
    return pl.pallas_call(
        functools.partial(product_kernel, len(chunks)),
        out_shape=[jax.ShapeDtypeStruct((rows, 2 * units + EXTRA), F32)] * 2,
        in_specs=[pl.BlockSpec(memory_space=pltpu.SMEM)] + [vmem] * (len(chunks) + 4),
        out_specs=[vmem, vmem],
        compiler_params=pltpu.CompilerParams(vmem_limit_bytes=16 * 2**20),
        cost_estimate=pl.CostEstimate(
            flops=4 * rows * depth * units, bytes_accessed=4 * depth * units, transcendentals=0
        ),
        name="expert_products",
    )(place, *chunks, w_gate, w_up, gate_other, up_other)


def finish_kernel(width, *refs):
    own_sums, pair_sums, (hidden, flipped) = refs[:N], refs[N : 2 * N], refs[2 * N :]
    units = hidden.shape[1]
    rows = hidden.shape[0] // (N * N)
    for i in range(N):
        for j in range(N):
            own = own_sums[i][j * rows : (j + 1) * rows, :]
            pair = pair_sums[j][i * rows : (i + 1) * rows, :]
            square = own[:, 2 * units : 2 * units + 1] + pair[:, 2 * units : 2 * units + 1]
            mix = own[:, 2 * units + 1 : 2 * units + 2]
            factor = lax.rsqrt(square / width + 1e-06)
            both = (own[:, : 2 * units] + pair[:, : 2 * units]) * factor
            gate, up = both[:, :units], both[:, units:]
            acted = (gate / (1.0 + jnp.exp(-gate)) * up * mix).astype(BF)
            hidden[(i * N + j) * rows : (i * N + j + 1) * rows, :] = acted
            flipped[(j * N + i) * rows : (j * N + i + 1) * rows, :] = acted


def expert_finish(width, rows, own_sums, pair_sums):
    columns = own_sums[0][0].shape[1]
    units = (columns - EXTRA) // 2

    def sums_spec(item):
        index = item[1] // rows
        return pl.BlockSpec((rows, columns), lambda k: (index, 0))

    whole = pl.BlockSpec((N * rows, units), lambda k: (0, 0))
    sums = list(own_sums) + list(pair_sums)
    return pl.pallas_call(
        functools.partial(finish_kernel, width),
        out_shape=[jax.ShapeDtypeStruct((N * rows, units), BF)] * 2,
        grid=(1,),
        in_specs=[sums_spec(item) for item in sums],
        out_specs=[whole, whole],
        compiler_params=pltpu.CompilerParams(vmem_limit_bytes=16 * 2**20),
        name="expert_finish",
    )(*[item[0] for item in sums])


def plane_index(y, x, c):
    return (y % N * N + x % N) * 2 + c


def leading(block, offset):
    pairs = [
        (plane_index(y, x, c), plane_index(y + offset * (1 - c), x + offset * c, c))
        for y in range(N) for x in range(N) for c in range(2)
    ]
    return lax.ppermute(block, PLANE, pairs)


def trailing(block, offset):
    pairs = [
        (plane_index(y, x, c), plane_index(y + offset * c, x + offset * (1 - c), c))
        for y in range(N) for x in range(N) for c in range(2)
    ]
    return lax.ppermute(block, PLANE, pairs)


def upright(block, offset):
    return lax.ppermute(block, "z", [(i, (i + offset) % N) for i in range(N)])


def swap(block):
    return lax.ppermute(block, "c", [(0, 1), (1, 0)])


def rolled(block, shift, dim):
    return lax.dynamic_slice_in_dim(
        jnp.concatenate([block, block], dim), shift, block.shape[dim], dim
    )


def half(block, which, dim):
    size = block.shape[dim] // 2
    return lax.dynamic_slice_in_dim(block, which * size, size, dim)


def mm(a, b):
    return jnp.dot(a, b, preferred_element_type=F32)


def three_pieces(values):
    top = lax.reduce_precision(values, 8, 7)
    middle = lax.reduce_precision(values - top, 8, 7)
    return [top, middle, values - top - middle]


def scatter_axis(chunks, send):
    arrived = [send(chunks[k], k) for k in range(1, N)]
    total = chunks[0].astype(F32)
    for block in arrived:
        total = total + block.astype(F32)
    return total


def gather_axis(block, send):
    return [block] + [send(block, -k) for k in range(1, N)]


def local(
    hidden_in, queries, cache, lengths, value_up, out_proj, norm_gain, routes, route_weight,
    w_gate, w_up, w_down,
):
    zi, yi, xi, ci = (lax.axis_index(a) for a in AXES)
    other = 1 - ci
    width = hidden_in.shape[1]
    wide = width // 2
    part = wide // 2
    requests = hidden_in.shape[0]
    chip = 2 * requests

    def chip_rows(mine, theirs):
        return jnp.concatenate(
            [jnp.where(ci == 0, mine, theirs), jnp.where(ci == 0, theirs, mine)], 0
        )

    gain = lax.dynamic_slice_in_dim(norm_gain, ci * wide, wide, 0)

    experts = jnp.arange(EXPERTS, dtype=jnp.int32)
    dense = jnp.sum(
        jnp.where(routes[:, :, None] == experts, route_weight[:, :, None], 0.0), 1
    )
    pieces = jnp.concatenate(three_pieces(dense) + [jnp.zeros_like(dense)], 1).astype(BF)

    core = ci.astype(jnp.int32).reshape(1)
    ranks = N * N * 2
    latent = attend(lengths, queries, cache, ranks)
    regrouped = lax.all_to_all(latent, PLANE, split_axis=0, concat_axis=0, tiled=True)
    regrouped = regrouped.reshape(ranks * requests, -1, LAT)
    _, *weights = lax.optimization_barrier((latent, w_gate[0], w_up[0], out_proj))
    sent = [half(weights[0], other, 0), half(weights[1], other, 0)]
    proj_pair, proj_own = half(weights[2], other, 1), half(weights[2], ci, 1)
    gate_other, up_other = (swap(block) for block in sent)
    regrouped, proj_pair, proj_own, sent = lax.optimization_barrier(
        (regrouped, proj_pair, proj_own, sent)
    )
    head_out = jnp.einsum("thl,hlv->thv", regrouped, value_up, preferred_element_type=F32)
    head_out = head_out.astype(BF).reshape(N, N, chip, -1)
    head_out = rolled(rolled(head_out, yi, 0), xi, 1)
    flipped = head_out.swapaxes(0, 1)
    own_order = jnp.where(ci == 0, head_out, flipped).reshape(N * N * chip, -1)
    pair_order = jnp.where(ci == 0, flipped, head_out).reshape(N * N * chip, -1)
    sent = swap(project(pair_order, proj_pair, BF))
    partial, gate_other, up_other = lax.optimization_barrier(
        (project(own_order, proj_own, F32), gate_other, up_other)
    )
    partial = partial + sent.astype(F32)
    partial = partial.astype(BF).reshape(N, N * chip, wide)
    partial, down, hidden_in, pieces = lax.optimization_barrier(
        (partial, w_down[0], hidden_in, pieces)
    )
    chip_hidden = chip_rows(half(hidden_in, ci, 1), swap(half(hidden_in, other, 1)))
    chip_pieces = chip_rows(pieces, swap(pieces))
    down_sent = half(down, other, 1)
    partial = scatter_axis([partial[k] for k in range(N)], leading)
    partial, down_sent = lax.optimization_barrier((partial, down_sent))
    down_other = swap(down_sent)
    partial = partial.astype(BF).reshape(N, chip, wide)
    attended = scatter_axis([partial[k] for k in range(N)], trailing)
    residual = chip_hidden.astype(F32) + attended
    squares = jnp.sum(residual * residual, 1, keepdims=True)
    lane = jnp.arange(EXTRA, dtype=jnp.int32)
    extra = chip_pieces
    for place, piece in enumerate(three_pieces(squares)):
        extra = jnp.where(lane == 3 * EXPERTS + place, piece.astype(BF), extra)

    shard = jnp.concatenate([(residual * gain).astype(BF), extra], 1)
    shard = jnp.concatenate(gather_axis(shard, upright), 0)
    blocks = gather_axis(shard, trailing)
    near_a = jnp.concatenate(blocks[: N // 2], 0)
    near_b = jnp.concatenate(blocks[N // 2 :], 0)
    tied = near_a[:chip, :EXTRA] + near_b[:chip, :EXTRA]
    near_a, near_b, _ = lax.optimization_barrier((near_a, near_b, swap(tied)))
    before_a, after_b = leading(near_a, 1), leading(near_b, -1)
    before_b, after_a = leading(near_b, 1), leading(near_a, -1)

    place = jnp.stack([ci, plane_index(yi, xi, ci)]).astype(jnp.int32)

    def products(chunks):
        own, cross = expert_products(place, chunks, w_gate[0], w_up[0], gate_other, up_other)
        return own, swap(cross)

    sums_0 = products([near_a, near_b])
    before_a, after_b, _ = lax.optimization_barrier((before_a, after_b, sums_0[0]))
    far_a, far_b = leading(before_a, 1), leading(after_b, -1)
    sums_13 = products([after_a, after_b, before_a, before_b])
    sums_2 = products([far_a, far_b])
    own_sums, pair_sums = (
        [(sums_0[p], 0), (sums_13[p], 0), (sums_2[p], 0), (sums_13[p], near_a.shape[0] * 2)]
        for p in range(2)
    )
    hidden, flipped = expert_finish(width, near_a.shape[0] * 2, own_sums, pair_sums)
    theirs = swap(flipped)

    def products_down(picks, dtype):
        return down_products(picks, dtype, core, hidden, theirs, w_down[0], down_other)

    far = products_down([(2, 0), (2, 1)], BF)
    relay_a, relay_b = leading(far[0], 1), leading(far[1], -1)
    near = products_down([(1, 1), (3, 0)], BF)
    next_b, last_a = leading(near[0], 1), leading(near[1], -1)
    second = products_down([(1, 0), (3, 1), (0, 0), (0, 1)], F32)
    next_a = leading((second[0] + relay_a.astype(F32)).astype(BF), 1)
    last_b = leading((second[1] + relay_b.astype(F32)).astype(BF), -1)
    out_a = second[2] + last_a.astype(F32) + next_a.astype(F32)
    out_b = second[3] + next_b.astype(F32) + last_b.astype(F32)
    out = jnp.concatenate([out_a.astype(BF), out_b.astype(BF)], 1).reshape(N, N * chip, wide)
    out, _ = lax.optimization_barrier((out, swap(out[0, :chip, :EXTRA])))
    out = scatter_axis([out[k] for k in range(N)], trailing)
    out = out.astype(BF).reshape(N, chip, wide)
    routed = scatter_axis([out[k] for k in range(N)], upright)
    layer_out = (residual + routed).astype(BF).reshape(2, requests, wide)
    mine = lax.dynamic_index_in_dim(layer_out, ci, 0, keepdims=False)
    theirs = swap(lax.dynamic_index_in_dim(layer_out, other, 0, keepdims=False))
    left = jnp.where(ci == 0, mine, theirs)
    right = jnp.where(ci == 0, theirs, mine)
    return jnp.concatenate([left, right], 1)


def solution(mesh):
    torus = Mesh(mesh.devices.reshape(N, N, N, 2), AXES)
    in_specs = (
        P(AXES, None),
        P(AXES, None, None),
        P(AXES, None),
        P(AXES),
        P(PLANE, None, None),
        P(PLANE, None),
        P(),
        P(AXES, None),
        P(AXES, None),
        P(PLANE, None, "z"),
        P(PLANE, None, "z"),
        P(PLANE, "z", None),
    )
    return jax.shard_map(
        local, mesh=torus, in_specs=in_specs, out_specs=P(AXES, None), check_vma=False
    )
```
